32 devices in a mesh: groups: 2 (over x), frame: 16 (over z, y, core).
Axes of the slice: x: 2, y: 2, z: 4, core: 2. Of those that a mesh axis runs over, the one named last changes fastest.
Arguments:
- lowres: bfloat16 [32, 64, 128], P(('groups', 'frame')), parts along dimension 0, may hold values from -6 to 6
- noisy: bfloat16 [32, 8, 64, 128], P(('groups', 'frame')), parts along dimension 0, may hold values from -6 to 6
- starts: int32 [8], P('groups'), parts along dimension 0, may hold values from 0 to 8, as said below
- blend: int32 [8, 8], P('groups'), parts along dimension 0, may hold values from 1 to 4
- assign: int32 [32], P('groups'), parts along dimension 0, may hold values from 0 to 15, each once
- base_w: bfloat16 [3, 128, 128], replicated, may hold values from -0.3125 to 0.3125
- cond_w: bfloat16 [128, 128], replicated, may hold values from -0.5 to 0.5
- noise_w: bfloat16 [128, 128], replicated, may hold values from -0.5 to 0.5
- gains: float32 [3, 128], replicated, may hold values from 0.25 to 1.75
- tconv: float32 [3, 3, 128], replicated, may hold values from -3 to 3
- mlp_in: bfloat16 [3, 128, 512], replicated, may hold values from -0.5 to 0.5
- mlp_out: bfloat16 [3, 512, 128], replicated, may hold values from -0.25 to 0.25
Outputs:
- video: bfloat16 [32, 256, 128], P(('groups', 'frame')), parts along dimension 0
The draws below stay inside these ranges and needn't reach their ends.
There are 2 independent parts, one for each index of `groups`. The reference program is written for one: setup_inputs(seed, part) draws one part's arguments, and reference() takes and returns one part's arrays. A program takes and returns all parts, laid end to end along the dimension named above; an argument that names none is the same for every part. Nothing has to cross between parts.
Inputs may be any that keep to these rules, and one draw needn't show every extreme that they name: Window k covers frames starts[k] to starts[k] + 7; every frame lies in some window; the first window starts at 0 and the last at 8.
All inputs are finite; a program needn't handle non-finite values.
Results may differ from the reference program's by a relative error of at most 0.0059.
Values may be sent and summed in bfloat16 or wider, within the bound.
A program may use at most 64 MiB of HBM per device.

```python
import jax
import jax.numpy as jnp
from jax import lax

C = 128
HID = 512
L = 8
TILES = 4
LAYERS = 3
TP = 64
PL = 16
FRAMES = 16
NWIN = 4


def draw_starts(key, part):
    window_ids = jnp.arange(NWIN, dtype=jnp.int32)
    spaced = window_ids * (FRAMES - L) // (NWIN - 1)
    jitter = jax.random.randint(jax.random.fold_in(key, 17), (NWIN,), -2, 3)
    placed = jnp.clip(spaced + jitter, 0, FRAMES - L)
    placed = jnp.where(window_ids == 0, 0, placed)
    placed = jnp.where(window_ids == NWIN - 1, FRAMES - L, placed)
    return placed.astype(jnp.int32)


def place_ends(values, key, smallest, top_value):
    spot = [jax.random.randint(jax.random.fold_in(key, axis), (), 0, length) for axis, length in enumerate(values.shape)]
    longest = values.shape.index(max(values.shape))
    neighbour = spot[:longest] + [(spot[longest] + 1) % values.shape[longest]] + spot[longest + 1:]
    return values.at[tuple(spot)].set(smallest).at[tuple(neighbour)].set(top_value)


def block_levels(key, extent, split, smallest, top_value):
    def one(axis_at, parts):
        steps = jax.random.uniform(jax.random.fold_in(jax.random.fold_in(key, 6), axis_at), (parts,), jnp.float32, smallest / len(split), top_value / len(split))
        return jnp.repeat(jnp.exp(steps), extent[axis_at] // parts).reshape((-1,) + (1,) * (len(extent) - axis_at - 1))

    level = one(*split[0])
    for cut in split[1:]:
        level = level * one(*cut)
    return level


def noise(own_key, shape, spread, reach, split=(), held_as=jnp.bfloat16):
    level = block_levels(own_key, shape, split, -0.22, 0.18) if split else 1.0
    array = jax.random.normal(own_key, shape, jnp.float32) * spread * level
    return jnp.minimum(jnp.maximum(array, -reach), reach).astype(held_as)


def setup_inputs(seed: int = 0, part: int = 0) -> dict:
    key_list = jax.random.split(jax.random.key(seed), 13)
    part_splits = jax.random.split(jax.random.fold_in(key_list[12], part), 13)
    return {
        "lowres": noise(part_splits[0], (FRAMES, TILES * PL, C), 1.0, 6.0, ((0, 16),)),
        "noisy": noise(part_splits[1], (FRAMES, L, TP, C), 1.0, 6.0, ((0, 16),)),
        "starts": draw_starts(jax.random.fold_in(jax.random.fold_in(key_list[12], part), 71), part),
        "blend": place_ends(jax.random.randint(part_splits[3], (NWIN, L), 1, 5), jax.random.fold_in(part_splits[3], 1), 1, 4).astype(jnp.int32),
        "assign": jax.random.permutation(part_splits[4], FRAMES).astype(jnp.int32),
        "base_w": noise(key_list[5], (3, C, C), (3 * C) ** -0.5, 0.3125),
        "cond_w": noise(key_list[6], (C, C), C ** -0.5, 0.5),
        "noise_w": noise(key_list[7], (C, C), C ** -0.5, 0.5),
        "gains": jnp.clip(1.0 + 0.15 * jax.random.normal(key_list[8], (LAYERS, C), jnp.float32), 0.25, 1.75),
        "tconv": noise(key_list[9], (LAYERS, 3, C), 0.5, 3.0, (), jnp.float32),
        "mlp_in": noise(key_list[10], (LAYERS, C, HID), C ** -0.5, 0.5),
        "mlp_out": noise(key_list[11], (LAYERS, HID, C), HID ** -0.5, 0.25),
    }


def base_frames(lowres, base_w):
    zeros_frame = jnp.zeros_like(lowres[:1])
    before = jnp.concatenate([zeros_frame, lowres[:-1]], 0)
    behind = jnp.concatenate([lowres[1:], zeros_frame], 0)
    row_count = lowres.shape[0] * lowres.shape[1]
    channels = lowres.shape[2]
    total = jnp.dot(before.reshape(row_count, channels), base_w[0], preferred_element_type=jnp.float32)
    total = total + jnp.dot(lowres.reshape(row_count, channels), base_w[1], preferred_element_type=jnp.float32)
    total = total + jnp.dot(behind.reshape(row_count, channels), base_w[2], preferred_element_type=jnp.float32)
    result = lowres.astype(jnp.float32) + jax.nn.silu(total).reshape(lowres.shape)
    return result.astype(jnp.bfloat16)

def refine(cond, noisy_item, cond_w, noise_w, gains, tconv, mlp_in, mlp_out):
    frame_count, positions, channels = cond.shape
    row_count = frame_count * positions
    state = jnp.dot(cond.reshape(row_count, channels), cond_w, preferred_element_type=jnp.float32)
    state = state + jnp.dot(noisy_item.reshape(row_count, channels), noise_w, preferred_element_type=jnp.float32)
    for layer_id in range(gains.shape[0]):
        inverse = lax.rsqrt(lax.optimization_barrier(jnp.mean(state * state, axis=-1, keepdims=True)) + 1e-06)
        normed = (state * inverse * gains[layer_id]).reshape(frame_count, positions, channels)
        zeros_frame = jnp.zeros_like(normed[:1])
        before = jnp.concatenate([zeros_frame, normed[:-1]], 0)
        behind = jnp.concatenate([normed[1:], zeros_frame], 0)
        mixed_rows = normed + tconv[layer_id, 0] * before + tconv[layer_id, 1] * normed + tconv[layer_id, 2] * behind
        mixed_rows = mixed_rows.reshape(row_count, channels).astype(jnp.bfloat16)
        hidden = jax.nn.silu(jnp.dot(mixed_rows, mlp_in[layer_id], preferred_element_type=jnp.float32)).astype(jnp.bfloat16)
        state = state + jnp.dot(hidden, mlp_out[layer_id], preferred_element_type=jnp.float32)
    return state.astype(jnp.bfloat16).reshape(frame_count, positions, channels)

def reference(lowres, noisy, starts, blend, assign, base_w, cond_w, noise_w, gains, tconv, mlp_in, mlp_out):
    base_all = base_frames(lowres, base_w)
    tiled = base_all.reshape(FRAMES, TILES, PL, C)
    zero_index = jnp.zeros((), jnp.int32)

    def one_slot(totals, slot_id):
        item_id = assign[slot_id].astype(jnp.int32)
        window_id = (item_id // TILES).astype(jnp.int32)
        tile_id = (item_id % TILES).astype(jnp.int32)
        first = starts[window_id].astype(jnp.int32)
        window_tiles = lax.dynamic_slice(tiled, (first, tile_id, zero_index, zero_index), (L, 1, PL, C))[:, 0]
        cond = jnp.repeat(window_tiles, 4, axis=1)
        refined = refine(cond, noisy[slot_id], cond_w, noise_w, gains, tconv, mlp_in, mlp_out)
        factor = blend[window_id].astype(jnp.float32)
        current = lax.dynamic_slice(totals, (first, tile_id, zero_index, zero_index), (L, 1, TP, C))
        updated = current + (factor[:, None, None] * refined.astype(jnp.float32))[:, None]
        totals = lax.dynamic_update_slice(totals, updated, (first, tile_id, zero_index, zero_index))
        return (totals, None)
    totals = jnp.zeros((FRAMES, TILES, TP, C), jnp.float32)
    totals, _ = lax.scan(one_slot, totals, jnp.arange(FRAMES, dtype=jnp.int32))
    covered = (starts[:, None] + jnp.arange(L, dtype=jnp.int32)[None, :]).astype(jnp.int32)
    denom = jax.ops.segment_sum(blend.reshape(-1).astype(jnp.float32), covered.reshape(-1), FRAMES)
    video = totals / denom[:, None, None, None]
    return video.reshape(FRAMES, TILES * TP, C).astype(jnp.bfloat16)
```

```python
import functools

import jax
import jax.numpy as jnp
from jax import lax
from jax.experimental import pallas as pl
from jax.experimental.pallas import tpu as pltpu
from jax.sharding import PartitionSpec as P

AXIS = "frame"
UNROLL_UP_TO = 16


def each(count, body, carry=None):
    if count <= UNROLL_UP_TO:
        for index in range(count):
            carry = body(index, carry)
        return carry
    return lax.fori_loop(0, count, body, carry)


def kernel(
    chunks,
    lowres_hbm, noisy_hbm, starts_hbm, blend_hbm, assign_hbm, base_w_hbm, cond_w_hbm, noise_w_hbm,
    gains_hbm, tconv_hbm, mlp_in_hbm, mlp_out_hbm,
    out_ref,
    lowres, noisy, starts, blend, assign, base_w, cond_w, noise_w, gains, tconv, mlp_in, mlp_out,
    tile_out, tile_in, state_ref, lifted, refined, frames_out, frames_in, weights,
    load_sem, tile_send_sem, tile_recv_sem, frame_send_sem, frame_recv_sem,
):
    slots = assign.shape[0]
    windows, window_len = blend.shape
    tiles = slots // windows
    tile_pos, channels = noisy.shape[1], noisy.shape[2]
    low_pos = lowres.shape[1]
    ratio = tile_pos // low_pos
    layers = gains.shape[0]
    part = tile_pos // chunks
    me = lax.axis_index(AXIS)

    loads = {}
    for spot, (name, source, target) in enumerate((
        ("assign", assign_hbm, assign),
        ("lowres", lowres_hbm, lowres),
        ("starts", starts_hbm, starts),
        ("blend", blend_hbm, blend),
        ("noisy", noisy_hbm.at[0], noisy),
        ("noise_w", noise_w_hbm, noise_w),
        ("base_w", base_w_hbm, base_w),
        ("cond_w", cond_w_hbm, cond_w),
        ("gains", gains_hbm, gains),
        ("tconv", tconv_hbm, tconv),
        ("mlp_in", mlp_in_hbm, mlp_in),
        ("mlp_out", mlp_out_hbm, mlp_out),
    )):
        loads[name] = pltpu.make_async_copy(source, target, load_sem.at[spot])
        loads[name].start()

    def partner(step):
        half = slots // 2
        offset = half + (step + 1) // 2 * (1 - 2 * (step % 2))
        return lax.rem(me + offset + slots, slots)

    barrier = pltpu.get_barrier_semaphore()

    def greet(step, carry):
        pl.semaphore_signal(
            barrier, inc=1, device_id={AXIS: partner(step)}, device_id_type=pl.DeviceIdType.MESH
        )
        return carry

    each(slots - 1, greet)

    zero_tile = jnp.zeros((low_pos, channels), tile_in.dtype)
    tile_in[0] = zero_tile
    tile_in[slots + 1] = zero_tile
    loads["assign"].wait()
    loads["lowres"].wait()

    def tile_for(slot):
        return lowres[lax.rem(assign[slot], tiles)]

    def pick(slot, carry):
        tile_out[slot] = tile_for(slot)
        return carry

    each(slots, pick)
    tile_in[me + 1] = tile_for(me)

    pl.semaphore_wait(barrier, slots - 1)

    def send_tile(step, carry):
        there = partner(step)
        pltpu.make_async_remote_copy(
            src_ref=tile_out.at[there],
            dst_ref=tile_in.at[me + 1],
            send_sem=tile_send_sem,
            recv_sem=tile_recv_sem,
            device_id={AXIS: there},
            device_id_type=pl.DeviceIdType.MESH,
        ).start()
        return carry

    each(slots - 1, send_tile)

    loads["noisy"].wait()
    loads["noise_w"].wait()
    rows = window_len * tile_pos
    state_ref[...] = jnp.dot(
        noisy[...].reshape(rows, channels), noise_w[...], preferred_element_type=jnp.float32
    ).reshape(window_len, tile_pos, channels)

    loads["starts"].wait()
    loads["blend"].wait()

    def weigh(slot, total):
        item = assign[slot]
        window = lax.div(item, tiles)
        tile = lax.rem(item, tiles)
        offset = me - starts[window]
        inside = jnp.logical_and(offset >= 0, offset < window_len)
        value = blend[window, jnp.clip(offset, 0, window_len - 1)]
        value = jnp.where(inside, value, 0)
        for t in range(tiles):
            weights[slot * tiles + t] = jnp.where(tile == t, value, 0).astype(jnp.float32)
        return total + jnp.where(tile == 0, value, 0)

    denom = each(slots, weigh, jnp.int32(0)).astype(jnp.float32)
    start = starts[lax.div(assign[me], tiles)]

    loads["gains"].wait()
    loads["tconv"].wait()
    loads["base_w"].wait()
    loads["cond_w"].wait()
    pltpu.make_async_copy(
        tile_in.at[pl.ds(0, slots - 1)],
        tile_in.at[pl.ds(0, slots - 1)],
        tile_recv_sem,
    ).wait()

    low_rows = window_len * low_pos
    near = [tile_in[start + k] for k in range(window_len + 2)]
    seen = [jnp.concatenate(near[k : k + window_len], 0) for k in range(3)]
    total = jnp.dot(seen[0], base_w[0], preferred_element_type=jnp.float32)
    total = total + jnp.dot(seen[1], base_w[1], preferred_element_type=jnp.float32)
    total = total + jnp.dot(seen[2], base_w[2], preferred_element_type=jnp.float32)
    half = total * 0.5
    base = (seen[1].astype(jnp.float32) + (half + half * jnp.tanh(half))).astype(jnp.bfloat16)
    projected = jnp.dot(base, cond_w[...], preferred_element_type=jnp.float32)
    for r in range(ratio):
        lifted[pl.ds(r, low_rows, stride=ratio), :] = projected

    loads["mlp_in"].wait()
    loads["mlp_out"].wait()
    for c in range(chunks):
        span = pl.ds(c * part, part)
        state = state_ref[:, span, :] + lifted[...].reshape(window_len, tile_pos, channels)[
            :, c * part : (c + 1) * part
        ]
        zeros_frame = jnp.zeros((1, part, channels), jnp.float32)
        for layer in range(layers):
            inverse = lax.rsqrt(jnp.mean(state * state, axis=-1, keepdims=True) + 1e-06)
            plain = state * inverse
            gain = gains[pl.ds(layer, 1), :] * 0.5
            taps = tconv[layer]
            before = (taps[0:1] * gain).reshape(1, 1, channels)
            here = (gain + taps[1:2] * gain).reshape(1, 1, channels)
            behind = (taps[2:3] * gain).reshape(1, 1, channels)
            mixed = (
                here * plain
                + before * jnp.concatenate([zeros_frame, plain[:-1]], 0)
                + behind * jnp.concatenate([plain[1:], zeros_frame], 0)
            )
            mixed = mixed.reshape(window_len * part, channels).astype(jnp.bfloat16)
            half = jnp.dot(mixed, mlp_in[layer], preferred_element_type=jnp.float32)
            hidden = (half + half * jnp.tanh(half)).astype(jnp.bfloat16)
            state = state + jnp.dot(
                hidden, mlp_out[layer], preferred_element_type=jnp.float32
            ).reshape(window_len, part, channels)
        refined[c] = state.astype(jnp.bfloat16)

        def place(frame, carry, c=c):
            frames_out[c, frame] = refined[c, jnp.clip(frame - start, 0, window_len - 1)]
            return carry

        each(slots, place)
        frames_in[c, me] = refined[c, jnp.clip(me - start, 0, window_len - 1)]

        def send_frame(step, carry, c=c):
            there = partner(step)
            pltpu.make_async_remote_copy(
                src_ref=frames_out.at[c, there],
                dst_ref=frames_in.at[c, me],
                send_sem=frame_send_sem.at[c],
                recv_sem=frame_recv_sem.at[c],
                device_id={AXIS: there},
                device_id_type=pl.DeviceIdType.MESH,
            ).start()
            return carry

        each(slots - 1, send_frame)

    scale = jnp.full((1, channels), 1.0, jnp.float32) / jnp.full((1, channels), denom, jnp.float32)
    for c in range(chunks):
        arrived = frames_in.at[c, pl.ds(0, slots - 1)]
        pltpu.make_async_copy(arrived, arrived, frame_recv_sem.at[c]).wait()

        def add(slot, sums, c=c):
            value = frames_in[c, slot].astype(jnp.float32)
            return tuple(
                sums[t] + weights[slot * tiles + t] * value for t in range(tiles)
            )

        sums = each(slots, add, tuple(jnp.zeros((part, channels), jnp.float32) for _ in range(tiles)))
        for t in range(tiles):
            out_ref[0, pl.ds(t * tile_pos + c * part, part), :] = (sums[t] * scale).astype(
                out_ref.dtype
            )

    sent = tile_out.at[pl.ds(0, slots - 1)]
    pltpu.make_async_copy(sent, sent, tile_send_sem).wait()
    for c in range(chunks):
        sent = frames_out.at[c, pl.ds(0, slots - 1)]
        pltpu.make_async_copy(sent, sent, frame_send_sem.at[c]).wait()


def on_device(chunks, *args):
    (lowres, noisy, starts, blend, assign, base_w, cond_w, noise_w, gains, tconv, mlp_in,
     mlp_out) = args
    slots = assign.shape[0]
    windows = starts.shape[0]
    tiles = slots // windows
    _, window_len, tile_pos, channels = noisy.shape
    low_pos = lowres.shape[1] // tiles
    part = tile_pos // chunks
    half = jnp.bfloat16
    full = jnp.float32
    whole = jnp.int32
    return pl.pallas_call(
        functools.partial(kernel, chunks),
        out_shape=jax.ShapeDtypeStruct((1, tiles * tile_pos, channels), half),
        in_specs=[pl.BlockSpec(memory_space=pltpu.HBM)] * len(args),
        out_specs=pl.BlockSpec(memory_space=pltpu.VMEM),
        scratch_shapes=[
            pltpu.VMEM((tiles, low_pos, channels), half),
            pltpu.VMEM(noisy.shape[1:], half),
            pltpu.SMEM(starts.shape, whole),
            pltpu.SMEM(blend.shape, whole),
            pltpu.SMEM(assign.shape, whole),
            pltpu.VMEM(base_w.shape, half),
            pltpu.VMEM(cond_w.shape, half),
            pltpu.VMEM(noise_w.shape, half),
            pltpu.VMEM(gains.shape, full),
            pltpu.VMEM(tconv.shape, full),
            pltpu.VMEM(mlp_in.shape, half),
            pltpu.VMEM(mlp_out.shape, half),
            pltpu.VMEM((slots, low_pos, channels), half),
            pltpu.VMEM((slots + 2, low_pos, channels), half),
            pltpu.VMEM((window_len, tile_pos, channels), full),
            pltpu.VMEM((window_len * tile_pos, channels), full),
            pltpu.VMEM((chunks, window_len, part, channels), half),
            pltpu.VMEM((chunks, slots, part, channels), half),
            pltpu.VMEM((chunks, slots, part, channels), half),
            pltpu.SMEM((slots * tiles,), full),
            pltpu.SemaphoreType.DMA((len(args),)),
            pltpu.SemaphoreType.DMA,
            pltpu.SemaphoreType.DMA,
            pltpu.SemaphoreType.DMA((chunks,)),
            pltpu.SemaphoreType.DMA((chunks,)),
        ],
        compiler_params=pltpu.CompilerParams(
            collective_id=0, has_side_effects=True, vmem_limit_bytes=60 * 1024 * 1024
        ),
    )(lowres.reshape(tiles, low_pos, channels), *args[1:])


def solution(mesh):
    in_specs = (
        P(("groups", AXIS), None, None),
        P(("groups", AXIS), None, None, None),
        P("groups"),
        P("groups", None),
        P("groups"),
        P(),
        P(),
        P(),
        P(),
        P(),
        P(),
        P(),
    )
    out_specs = P(("groups", AXIS), None, None)
    return jax.shard_map(
        functools.partial(on_device, 2),
        mesh=mesh, in_specs=in_specs, out_specs=out_specs, check_vma=False
    )
```

```python
import functools

import jax
import jax.numpy as jnp
from jax import lax
from jax.experimental import pallas as pl
from jax.experimental.pallas import tpu as pltpu
from jax.sharding import PartitionSpec as P

AXIS = "frame"
UNROLL_UP_TO = 16


def each(count, body, carry=None):
    if count <= UNROLL_UP_TO:
        for index in range(count):
            carry = body(index, carry)
        return carry
    return lax.fori_loop(0, count, body, carry)


def kernel(
    chunks,
    lowres_hbm, noisy_hbm, starts_hbm, blend_hbm, assign_hbm, base_w_hbm, cond_w_hbm, noise_w_hbm,
    gains_hbm, tconv_hbm, mlp_in_hbm, mlp_out_hbm,
    out_ref,
    lowres, noisy, starts, blend, assign, base_w, cond_w, noise_w, gains, tconv, mlp_in, mlp_out,
    tile_out, tile_in, state_ref, lifted, refined, frames_out, frames_in, weights,
    load_sem, tile_send_sem, tile_recv_sem, frame_send_sem, frame_recv_sem,
):
    slots = assign.shape[0]
    windows, window_len = blend.shape
    tiles = slots // windows
    tile_pos, channels = noisy.shape[1], noisy.shape[2]
    low_pos = lowres.shape[1]
    ratio = tile_pos // low_pos
    layers = gains.shape[0]
    part = tile_pos // chunks
    me = lax.axis_index(AXIS)

    loads = {}
    for spot, (name, source, target) in enumerate((
        ("assign", assign_hbm, assign),
        ("lowres", lowres_hbm, lowres),
        ("starts", starts_hbm, starts),
        ("blend", blend_hbm, blend),
        ("noisy", noisy_hbm.at[0], noisy),
        ("noise_w", noise_w_hbm, noise_w),
        ("base_w", base_w_hbm, base_w),
        ("cond_w", cond_w_hbm, cond_w),
        ("gains", gains_hbm, gains),
        ("tconv", tconv_hbm, tconv),
        ("mlp_in", mlp_in_hbm, mlp_in),
        ("mlp_out", mlp_out_hbm, mlp_out),
    )):
        loads[name] = pltpu.make_async_copy(source, target, load_sem.at[spot])
        loads[name].start()

    def partner(step):
        half = slots // 2
        offset = half + (step + 1) // 2 * (1 - 2 * (step % 2))
        return lax.rem(me + offset + slots, slots)

    barrier = pltpu.get_barrier_semaphore()

    def greet(step, carry):
        pl.semaphore_signal(
            barrier, inc=1, device_id={AXIS: partner(step)}, device_id_type=pl.DeviceIdType.MESH
        )
        return carry

    each(slots - 1, greet)

    zero_tile = jnp.zeros((low_pos, channels), tile_in.dtype)
    tile_in[0] = zero_tile
    tile_in[slots + 1] = zero_tile
    loads["assign"].wait()
    loads["lowres"].wait()

    def tile_for(slot):
        return lowres[lax.rem(assign[slot], tiles)]

    def pick(slot, carry):
        tile_out[slot] = tile_for(slot)
        return carry

    each(slots, pick)
    tile_in[me + 1] = tile_for(me)

    pl.semaphore_wait(barrier, slots - 1)

    def send_tile(step, carry):
        there = partner(step)
        pltpu.make_async_remote_copy(
            src_ref=tile_out.at[there],
            dst_ref=tile_in.at[me + 1],
            send_sem=tile_send_sem,
            recv_sem=tile_recv_sem,
            device_id={AXIS: there},
            device_id_type=pl.DeviceIdType.MESH,
        ).start()
        return carry

    each(slots - 1, send_tile)

    loads["noisy"].wait()
    loads["noise_w"].wait()
    rows = window_len * tile_pos
    state_ref[...] = jnp.dot(
        noisy[...].reshape(rows, channels), noise_w[...], preferred_element_type=jnp.float32
    ).reshape(window_len, tile_pos, channels)

    loads["starts"].wait()
    loads["blend"].wait()

    def weigh(slot, total):
        item = assign[slot]
        window = lax.div(item, tiles)
        tile = lax.rem(item, tiles)
        offset = me - starts[window]
        inside = jnp.logical_and(offset >= 0, offset < window_len)
        value = blend[window, jnp.clip(offset, 0, window_len - 1)]
        value = jnp.where(inside, value, 0)
        for t in range(tiles):
            weights[slot * tiles + t] = jnp.where(tile == t, value, 0).astype(jnp.float32)
        return total + jnp.where(tile == 0, value, 0)

    denom = each(slots, weigh, jnp.int32(0)).astype(jnp.float32)
    start = starts[lax.div(assign[me], tiles)]

    loads["gains"].wait()
    loads["tconv"].wait()
    loads["base_w"].wait()
    loads["cond_w"].wait()
    pltpu.make_async_copy(
        tile_in.at[pl.ds(0, slots - 1)],
        tile_in.at[pl.ds(0, slots - 1)],
        tile_recv_sem,
    ).wait()

    low_rows = window_len * low_pos
    near = [tile_in[start + k] for k in range(window_len + 2)]
    seen = [jnp.concatenate(near[k : k + window_len], 0) for k in range(3)]
    total = jnp.dot(seen[0], base_w[0], preferred_element_type=jnp.float32)
    total = total + jnp.dot(seen[1], base_w[1], preferred_element_type=jnp.float32)
    total = total + jnp.dot(seen[2], base_w[2], preferred_element_type=jnp.float32)
    half = total * 0.5
    base = (seen[1].astype(jnp.float32) + (half + half * jnp.tanh(half))).astype(jnp.bfloat16)
    projected = jnp.dot(base, cond_w[...], preferred_element_type=jnp.float32)
    for r in range(ratio):
        lifted[pl.ds(r, low_rows, stride=ratio), :] = projected

    loads["mlp_in"].wait()
    loads["mlp_out"].wait()
    for c in range(chunks):
        span = pl.ds(c * part, part)
        state = state_ref[:, span, :] + lifted[...].reshape(window_len, tile_pos, channels)[
            :, c * part : (c + 1) * part
        ]
        zeros_frame = jnp.zeros((1, part, channels), jnp.float32)
        for layer in range(layers):
            inverse = lax.rsqrt(jnp.mean(state * state, axis=-1, keepdims=True) + 1e-06)
            plain = state * inverse
            gain = gains[pl.ds(layer, 1), :] * 0.5
            taps = tconv[layer]
            before = (taps[0:1] * gain).reshape(1, 1, channels)
            here = (gain + taps[1:2] * gain).reshape(1, 1, channels)
            behind = (taps[2:3] * gain).reshape(1, 1, channels)
            mixed = (
                here * plain
                + before * jnp.concatenate([zeros_frame, plain[:-1]], 0)
                + behind * jnp.concatenate([plain[1:], zeros_frame], 0)
            )
            mixed = mixed.reshape(window_len * part, channels).astype(jnp.bfloat16)
            half = jnp.dot(mixed, mlp_in[layer], preferred_element_type=jnp.float32)
            hidden = (half + half * jnp.tanh(half)).astype(jnp.bfloat16)
            state = state + jnp.dot(
                hidden, mlp_out[layer], preferred_element_type=jnp.float32
            ).reshape(window_len, part, channels)
        refined[c] = state.astype(jnp.bfloat16)

        def place(frame, carry, c=c):
            frames_out[c, frame] = refined[c, jnp.clip(frame - start, 0, window_len - 1)]
            return carry

        each(slots, place)
        frames_in[c, me] = refined[c, jnp.clip(me - start, 0, window_len - 1)]

        def send_frame(step, carry, c=c):
            there = partner(step)
            pltpu.make_async_remote_copy(
                src_ref=frames_out.at[c, there],
                dst_ref=frames_in.at[c, me],
                send_sem=frame_send_sem.at[c],
                recv_sem=frame_recv_sem.at[c],
                device_id={AXIS: there},
                device_id_type=pl.DeviceIdType.MESH,
            ).start()
            return carry

        each(slots - 1, send_frame)

    scale = jnp.full((1, channels), 1.0, jnp.float32) / jnp.full((1, channels), denom, jnp.float32)
    for c in range(chunks):
        arrived = frames_in.at[c, pl.ds(0, slots - 1)]
        pltpu.make_async_copy(arrived, arrived, frame_recv_sem.at[c]).wait()

        def add(slot, sums, c=c):
            value = frames_in[c, slot].astype(jnp.float32)
            return tuple(
                sums[t] + weights[slot * tiles + t] * value for t in range(tiles)
            )

        sums = each(slots, add, tuple(jnp.zeros((part, channels), jnp.float32) for _ in range(tiles)))
        for t in range(tiles):
            out_ref[0, pl.ds(t * tile_pos + c * part, part), :] = (sums[t] * scale).astype(
                out_ref.dtype
            )

    sent = tile_out.at[pl.ds(0, slots - 1)]
    pltpu.make_async_copy(sent, sent, tile_send_sem).wait()
    for c in range(chunks):
        sent = frames_out.at[c, pl.ds(0, slots - 1)]
        pltpu.make_async_copy(sent, sent, frame_send_sem.at[c]).wait()


def on_device(chunks, *args):
    (lowres, noisy, starts, blend, assign, base_w, cond_w, noise_w, gains, tconv, mlp_in,
     mlp_out) = args
    slots = assign.shape[0]
    windows = starts.shape[0]
    tiles = slots // windows
    _, window_len, tile_pos, channels = noisy.shape
    low_pos = lowres.shape[1] // tiles
    part = tile_pos // chunks
    half = jnp.bfloat16
    full = jnp.float32
    whole = jnp.int32
    return pl.pallas_call(
        functools.partial(kernel, chunks),
        out_shape=jax.ShapeDtypeStruct((1, tiles * tile_pos, channels), full),
        in_specs=[pl.BlockSpec(memory_space=pltpu.HBM)] * len(args),
        out_specs=pl.BlockSpec(memory_space=pltpu.VMEM),
        scratch_shapes=[
            pltpu.VMEM((tiles, low_pos, channels), half),
            pltpu.VMEM(noisy.shape[1:], half),
            pltpu.SMEM(starts.shape, whole),
            pltpu.SMEM(blend.shape, whole),
            pltpu.SMEM(assign.shape, whole),
            pltpu.VMEM(base_w.shape, half),
            pltpu.VMEM(cond_w.shape, half),
            pltpu.VMEM(noise_w.shape, half),
            pltpu.VMEM(gains.shape, full),
            pltpu.VMEM(tconv.shape, full),
            pltpu.VMEM(mlp_in.shape, half),
            pltpu.VMEM(mlp_out.shape, half),
            pltpu.VMEM((slots, low_pos, channels), half),
            pltpu.VMEM((slots + 2, low_pos, channels), half),
            pltpu.VMEM((window_len, tile_pos, channels), full),
            pltpu.VMEM((window_len * tile_pos, channels), full),
            pltpu.VMEM((chunks, window_len, part, channels), half),
            pltpu.VMEM((chunks, slots, part, channels), half),
            pltpu.VMEM((chunks, slots, part, channels), half),
            pltpu.SMEM((slots * tiles,), full),
            pltpu.SemaphoreType.DMA((len(args),)),
            pltpu.SemaphoreType.DMA,
            pltpu.SemaphoreType.DMA,
            pltpu.SemaphoreType.DMA((chunks,)),
            pltpu.SemaphoreType.DMA((chunks,)),
        ],
        compiler_params=pltpu.CompilerParams(
            collective_id=0, has_side_effects=True, vmem_limit_bytes=60 * 1024 * 1024
        ),
    )(lowres.reshape(tiles, low_pos, channels), *args[1:]).astype(half)


def solution(mesh):
    in_specs = (
        P(("groups", AXIS), None, None),
        P(("groups", AXIS), None, None, None),
        P("groups"),
        P("groups", None),
        P("groups"),
        P(),
        P(),
        P(),
        P(),
        P(),
        P(),
        P(),
    )
    out_specs = P(("groups", AXIS), None, None)
    return jax.shard_map(
        functools.partial(on_device, 4),
        mesh=mesh, in_specs=in_specs, out_specs=out_specs, check_vma=False
    )
```

```python
import functools

import jax
import jax.numpy as jnp
from jax import lax
from jax.experimental import pallas as pl
from jax.experimental.pallas import tpu as pltpu
from jax.sharding import PartitionSpec as P

AXIS = "frame"
UNROLL_UP_TO = 16
SUBLANES = 8


def each(count, body, carry=None):
    if count <= UNROLL_UP_TO:
        for index in range(count):
            carry = body(index, carry)
        return carry
    return lax.fori_loop(0, count, body, carry)


def slot_kernel(
    chunks,
    lowres_hbm, noisy_hbm, starts_hbm, blend_hbm, assign_hbm, base_w_hbm, cond_w_hbm, noise_w_hbm,
    gains_hbm, tconv_hbm, mlp_in_hbm, mlp_out_hbm,
    out_ref,
    lowres, noisy, starts, blend, assign, base_w, cond_w, noise_w, gains, tconv, mlp_in, mlp_out,
    tile_out, tile_in, state_ref, lifted, refined, frames_out, frames_in, weights,
    load_sem, tile_send_sem, tile_recv_sem, frame_send_sem, frame_recv_sem,
):
    slots = assign.shape[0]
    windows, window_len = blend.shape
    tiles = slots // windows
    tile_pos, channels = noisy.shape[1], noisy.shape[2]
    low_pos = lowres.shape[1]
    ratio = tile_pos // low_pos
    layers = gains.shape[0]
    part = tile_pos // chunks
    me = lax.axis_index(AXIS)

    loads = {}
    for spot, (name, source, target) in enumerate((
        ("assign", assign_hbm, assign),
        ("lowres", lowres_hbm, lowres),
        ("starts", starts_hbm, starts),
        ("blend", blend_hbm, blend),
        ("noisy", noisy_hbm.at[0], noisy),
        ("noise_w", noise_w_hbm, noise_w),
        ("base_w", base_w_hbm, base_w),
        ("cond_w", cond_w_hbm, cond_w),
        ("gains", gains_hbm, gains),
        ("tconv", tconv_hbm, tconv),
        ("mlp_in", mlp_in_hbm, mlp_in),
        ("mlp_out", mlp_out_hbm, mlp_out),
    )):
        loads[name] = pltpu.make_async_copy(source, target, load_sem.at[spot])
        loads[name].start()

    def partner(step):
        half = slots // 2
        offset = half + (step + 1) // 2 * (1 - 2 * (step % 2))
        return lax.rem(me + offset + slots, slots)

    barrier = pltpu.get_barrier_semaphore()

    def greet(step, carry):
        pl.semaphore_signal(
            barrier, inc=1, device_id={AXIS: partner(step)}, device_id_type=pl.DeviceIdType.MESH
        )
        return carry

    each(slots - 1, greet)

    zero_tile = jnp.zeros((low_pos, channels), tile_in.dtype)
    tile_in[0] = zero_tile
    tile_in[slots + 1] = zero_tile
    loads["assign"].wait()
    loads["lowres"].wait()

    def tile_for(slot):
        return lowres[lax.rem(assign[slot], tiles)]

    def pick(slot, carry):
        tile_out[slot] = tile_for(slot)
        return carry

    each(slots, pick)
    tile_in[me + 1] = tile_for(me)

    pl.semaphore_wait(barrier, slots - 1)

    def send_tile(step, carry):
        there = partner(step)
        pltpu.make_async_remote_copy(
            src_ref=tile_out.at[there],
            dst_ref=tile_in.at[me + 1],
            send_sem=tile_send_sem,
            recv_sem=tile_recv_sem,
            device_id={AXIS: there},
            device_id_type=pl.DeviceIdType.MESH,
        ).start()
        return carry

    each(slots - 1, send_tile)

    loads["noisy"].wait()
    loads["noise_w"].wait()
    rows = window_len * tile_pos
    state_ref[...] = jnp.dot(
        noisy[...].reshape(rows, channels), noise_w[...], preferred_element_type=jnp.float32
    ).reshape(window_len, tile_pos, channels)

    loads["starts"].wait()
    loads["blend"].wait()

    def weigh(slot, total):
        item = assign[slot]
        window = lax.div(item, tiles)
        tile = lax.rem(item, tiles)
        offset = me - starts[window]
        inside = jnp.logical_and(offset >= 0, offset < window_len)
        value = blend[window, jnp.clip(offset, 0, window_len - 1)]
        value = jnp.where(inside, value, 0)
        for t in range(tiles):
            weights[slot * tiles + t] = jnp.where(tile == t, value, 0).astype(jnp.float32)
        return total + jnp.where(tile == 0, value, 0)

    denom = each(slots, weigh, jnp.int32(0)).astype(jnp.float32)
    start = starts[lax.div(assign[me], tiles)]

    loads["gains"].wait()
    loads["tconv"].wait()
    loads["base_w"].wait()
    loads["cond_w"].wait()
    pltpu.make_async_copy(
        tile_in.at[pl.ds(0, slots - 1)],
        tile_in.at[pl.ds(0, slots - 1)],
        tile_recv_sem,
    ).wait()

    low_rows = window_len * low_pos
    near = [tile_in[start + k] for k in range(window_len + 2)]
    seen = [jnp.concatenate(near[k : k + window_len], 0) for k in range(3)]
    total = jnp.dot(seen[0], base_w[0], preferred_element_type=jnp.float32)
    total = total + jnp.dot(seen[1], base_w[1], preferred_element_type=jnp.float32)
    total = total + jnp.dot(seen[2], base_w[2], preferred_element_type=jnp.float32)
    half = total * 0.5
    base = (seen[1].astype(jnp.float32) + (half + half * jnp.tanh(half))).astype(jnp.bfloat16)
    projected = jnp.dot(base, cond_w[...], preferred_element_type=jnp.float32)
    for r in range(ratio):
        lifted[pl.ds(r, low_rows, stride=ratio), :] = projected

    loads["mlp_in"].wait()
    loads["mlp_out"].wait()
    for c in range(chunks):
        span = pl.ds(c * part, part)
        state = state_ref[:, span, :] + lifted[...].reshape(window_len, tile_pos, channels)[
            :, c * part : (c + 1) * part
        ]
        zeros_frame = jnp.zeros((1, part, channels), jnp.float32)
        for layer in range(layers):
            inverse = lax.rsqrt(jnp.mean(state * state, axis=-1, keepdims=True) + 1e-06)
            plain = state * inverse
            gain = gains[pl.ds(layer, 1), :] * 0.5
            taps = tconv[layer]
            before = (taps[0:1] * gain).reshape(1, 1, channels)
            here = (gain + taps[1:2] * gain).reshape(1, 1, channels)
            behind = (taps[2:3] * gain).reshape(1, 1, channels)
            mixed = (
                here * plain
                + before * jnp.concatenate([zeros_frame, plain[:-1]], 0)
                + behind * jnp.concatenate([plain[1:], zeros_frame], 0)
            )
            mixed = mixed.reshape(window_len * part, channels).astype(jnp.bfloat16)
            half = jnp.dot(mixed, mlp_in[layer], preferred_element_type=jnp.float32)
            hidden = (half + half * jnp.tanh(half)).astype(jnp.bfloat16)
            state = state + jnp.dot(
                hidden, mlp_out[layer], preferred_element_type=jnp.float32
            ).reshape(window_len, part, channels)
        refined[c] = state.astype(jnp.bfloat16)

        def place(frame, carry, c=c):
            frames_out[c, frame] = refined[c, jnp.clip(frame - start, 0, window_len - 1)]
            return carry

        each(slots, place)
        frames_in[c, me] = refined[c, jnp.clip(me - start, 0, window_len - 1)]

        def send_frame(step, carry, c=c):
            there = partner(step)
            pltpu.make_async_remote_copy(
                src_ref=frames_out.at[c, there],
                dst_ref=frames_in.at[c, me],
                send_sem=frame_send_sem.at[c],
                recv_sem=frame_recv_sem.at[c],
                device_id={AXIS: there},
                device_id_type=pl.DeviceIdType.MESH,
            ).start()
            return carry

        each(slots - 1, send_frame)

    scale = jnp.full((1, channels), 1.0, jnp.float32) / jnp.full((1, channels), denom, jnp.float32)
    for c in range(chunks):
        arrived = frames_in.at[c, pl.ds(0, slots - 1)]
        pltpu.make_async_copy(arrived, arrived, frame_recv_sem.at[c]).wait()

        def add(slot, sums, c=c):
            value = frames_in[c, slot].astype(jnp.float32)
            return tuple(
                sums[t] + weights[slot * tiles + t] * value for t in range(tiles)
            )

        sums = each(slots, add, tuple(jnp.zeros((part, channels), jnp.float32) for _ in range(tiles)))
        for t in range(tiles):
            out_ref[0, pl.ds(t * tile_pos + c * part, part), :] = (sums[t] * scale).astype(
                out_ref.dtype
            )

    sent = tile_out.at[pl.ds(0, slots - 1)]
    pltpu.make_async_copy(sent, sent, tile_send_sem).wait()
    for c in range(chunks):
        sent = frames_out.at[c, pl.ds(0, slots - 1)]
        pltpu.make_async_copy(sent, sent, frame_send_sem.at[c]).wait()


def slot_on_device(chunks, *args):
    (lowres, noisy, starts, blend, assign, base_w, cond_w, noise_w, gains, tconv, mlp_in,
     mlp_out) = args
    slots = assign.shape[0]
    windows = starts.shape[0]
    tiles = slots // windows
    _, window_len, tile_pos, channels = noisy.shape
    low_pos = lowres.shape[1] // tiles
    part = tile_pos // chunks
    half = jnp.bfloat16
    full = jnp.float32
    whole = jnp.int32
    return pl.pallas_call(
        functools.partial(slot_kernel, chunks),
        out_shape=jax.ShapeDtypeStruct((1, tiles * tile_pos, channels), half),
        in_specs=[pl.BlockSpec(memory_space=pltpu.HBM)] * len(args),
        out_specs=pl.BlockSpec(memory_space=pltpu.VMEM),
        scratch_shapes=[
            pltpu.VMEM((tiles, low_pos, channels), half),
            pltpu.VMEM(noisy.shape[1:], half),
            pltpu.SMEM(starts.shape, whole),
            pltpu.SMEM(blend.shape, whole),
            pltpu.SMEM(assign.shape, whole),
            pltpu.VMEM(base_w.shape, half),
            pltpu.VMEM(cond_w.shape, half),
            pltpu.VMEM(noise_w.shape, half),
            pltpu.VMEM(gains.shape, full),
            pltpu.VMEM(tconv.shape, full),
            pltpu.VMEM(mlp_in.shape, half),
            pltpu.VMEM(mlp_out.shape, half),
            pltpu.VMEM((slots, low_pos, channels), half),
            pltpu.VMEM((slots + 2, low_pos, channels), half),
            pltpu.VMEM((window_len, tile_pos, channels), full),
            pltpu.VMEM((window_len * tile_pos, channels), full),
            pltpu.VMEM((chunks, window_len, part, channels), half),
            pltpu.VMEM((chunks, slots, part, channels), half),
            pltpu.VMEM((chunks, slots, part, channels), half),
            pltpu.SMEM((slots * tiles,), full),
            pltpu.SemaphoreType.DMA((len(args),)),
            pltpu.SemaphoreType.DMA,
            pltpu.SemaphoreType.DMA,
            pltpu.SemaphoreType.DMA((chunks,)),
            pltpu.SemaphoreType.DMA((chunks,)),
        ],
        compiler_params=pltpu.CompilerParams(
            collective_id=0, has_side_effects=True, vmem_limit_bytes=60 * 1024 * 1024
        ),
    )(lowres.reshape(tiles, low_pos, channels), *args[1:])


def split_kernel(
    lowres_hbm, noisy_hbm, starts_hbm, blend_hbm, assign_hbm, base_w_hbm, cond_w_hbm, noise_w_hbm,
    gains_hbm, tconv_hbm, mlp_in_hbm, mlp_out_hbm,
    out_ref,
    lowres, noisy, starts, blend, assign, base_w, cond_w, noise_w, gains, tconv, mlp_in, mlp_out,
    low_out, low_in, noisy_wide, noisy_out, noisy_in, projected, shifted, cond_ref,
    video_out, video_in, video_wide,
    load_sem, low_send, low_recv, noisy_send, noisy_recv, video_send, video_recv,
):
    slots = assign.shape[0]
    windows, window_len = blend.shape
    tiles, low_pos, channels = lowres.shape
    tile_pos = noisy.shape[1]
    ratio = tile_pos // low_pos
    layers = gains.shape[0]
    pad = low_out.shape[0] // slots
    me = lax.axis_index(AXIS)

    loads = {}
    for spot, (name, source, target) in enumerate((
        ("lowres", lowres_hbm, lowres),
        ("noisy", noisy_hbm.at[0], noisy),
        ("assign", assign_hbm, assign),
        ("starts", starts_hbm, starts),
        ("blend", blend_hbm, blend),
        ("base_w", base_w_hbm, base_w),
        ("cond_w", cond_w_hbm, cond_w),
        ("noise_w", noise_w_hbm, noise_w),
        ("gains", gains_hbm, gains),
        ("tconv", tconv_hbm, tconv),
        ("mlp_in", mlp_in_hbm, mlp_in),
        ("mlp_out", mlp_out_hbm, mlp_out),
    )):
        loads[name] = pltpu.make_async_copy(source, target, load_sem.at[spot])
        loads[name].start()

    partners = []
    for step in range(slots - 1):
        offset = slots // 2 + (step + 1) // 2 * (1 - 2 * (step % 2))
        partners.append(lax.rem(me + offset, slots))

    barrier = pltpu.get_barrier_semaphore()
    for there in partners:
        pl.semaphore_signal(
            barrier, inc=1, device_id={AXIS: there}, device_id_type=pl.DeviceIdType.MESH
        )

    def send(source, target, there, send_sem, recv_sem):
        pltpu.make_async_remote_copy(
            src_ref=source, dst_ref=target, send_sem=send_sem, recv_sem=recv_sem,
            device_id={AXIS: there}, device_id_type=pl.DeviceIdType.MESH,
        ).start()

    def await_bytes(ref, sem):
        pltpu.make_async_copy(ref, ref, sem).wait()

    def block(index, rows):
        return pl.ds(pl.multiple_of(index * rows, rows), rows)

    low_out[...] = jnp.zeros_like(low_out)
    zero_pad = jnp.zeros((pad, channels), jnp.float32)
    low_in[pl.ds(0, pad), :] = zero_pad
    low_in[pl.ds((slots + 1) * pad, pad), :] = zero_pad
    loads["lowres"].wait()
    for t in range(tiles):
        low_out[pl.ds(t, low_pos, stride=pad), :] = lowres[t].astype(jnp.float32)
    low_in[block(me + 1, pad), :] = low_out[block(me, pad), :]

    loads["noisy"].wait()
    noisy_wide[...] = noisy[...].reshape(window_len * tile_pos, channels).astype(jnp.float32)
    for j in range(slots):
        picked = [
            noisy_wide[pl.ds(j * ratio + r, window_len, stride=tile_pos), :] for r in range(ratio)
        ]
        noisy_out[j] = jnp.concatenate(picked, 0).astype(jnp.bfloat16)
    noisy_in[me] = noisy_out[me]

    pl.semaphore_wait(barrier, slots - 1)
    for there in partners:
        send(low_out.at[block(there, pad)], low_in.at[block(me + 1, pad)], there, low_send, low_recv)
    for there in partners:
        send(noisy_out.at[there], noisy_in.at[me], there, noisy_send, noisy_recv)

    for name in ("assign", "starts", "blend"):
        loads[name].wait()
    rows = slots * ratio * window_len
    lane = lax.broadcasted_iota(jnp.int32, (1, rows), 1)
    lane_slot = lane // (ratio * window_len)
    lane_pos = (lane // window_len) % ratio
    lane_step = lane % window_len
    first = jnp.zeros((1, rows), jnp.int32)
    lane_tile = jnp.zeros((1, rows), jnp.int32)
    lane_window = jnp.zeros((1, rows), jnp.int32)
    for d in range(slots):
        item = assign[d]
        here = lane_slot == d
        window = lax.div(item, tiles)
        lane_window = jnp.where(here, window, lane_window)
        lane_tile = jnp.where(here, lax.rem(item, tiles), lane_tile)
        first = jnp.where(here, starts[window], first)
    factor = jnp.zeros((1, rows), jnp.int32)
    for w in range(windows):
        for k in range(window_len):
            factor = jnp.where(
                jnp.logical_and(lane_window == w, lane_step == k), blend[w, k], factor
            )
    target = ((first + lane_step) * tiles + lane_tile) * ratio + lane_pos
    video_rows = slots * tiles * ratio
    row = lax.broadcasted_iota(jnp.int32, (video_rows, rows), 0)
    matrix = jnp.where(row == target, factor.astype(jnp.float32), 0.0)
    denom = jnp.sum(matrix, axis=1, keepdims=True)
    matrix = matrix.astype(jnp.bfloat16)

    for name in ("base_w", "cond_w", "noise_w", "gains", "tconv"):
        loads[name].wait()
    await_bytes(low_in.at[pl.ds(0, (slots - 1) * pad)], low_recv)
    total = None
    for k in range(3):
        seen = jnp.concatenate(
            [low_in[pl.ds(k * pad + t, slots, stride=pad), :] for t in range(tiles)], 0
        )
        if k == 1:
            centre = seen
        term = jnp.dot(seen.astype(jnp.bfloat16), base_w[k], preferred_element_type=jnp.float32)
        total = term if total is None else total + term
    half = total * 0.5
    base = (centre + (half + half * jnp.tanh(half))).astype(jnp.bfloat16)
    projected[...] = jnp.dot(base, cond_w[...], preferred_element_type=jnp.float32)
    for t in range(tiles):
        for f in range(slots - window_len + 1):
            shifted[t, f] = projected[pl.ds(t * slots + f, window_len), :]
    for d in range(slots):
        item = assign[d]
        cond_ref[d, 0] = shifted[lax.rem(item, tiles), starts[lax.div(item, tiles)]]

    loads["mlp_in"].wait()
    loads["mlp_out"].wait()
    await_bytes(noisy_in.at[pl.ds(0, slots - 1)], noisy_recv)
    state = jnp.dot(
        noisy_in[...].reshape(rows, channels), noise_w[...], preferred_element_type=jnp.float32
    ).reshape(slots, ratio, window_len, channels)
    state = (state + cond_ref[...]).reshape(slots * ratio, window_len, channels)
    step_row = lax.broadcasted_iota(jnp.int32, (window_len, channels), 0)
    for layer in range(layers):
        inverse = lax.rsqrt(jnp.mean(state * state, axis=-1, keepdims=True) + 1e-06)
        plain = state * inverse
        gain = gains[pl.ds(layer, 1), :] * 0.5
        taps = tconv[layer]
        before = jnp.where(step_row == 0, 0.0, taps[0:1] * gain)
        here = gain + taps[1:2] * gain
        behind = jnp.where(step_row == window_len - 1, 0.0, taps[2:3] * gain)
        mixed = (
            here[None] * plain
            + before[None] * pltpu.roll(plain, 1, 1)
            + behind[None] * pltpu.roll(plain, window_len - 1, 1)
        )
        mixed = mixed.reshape(rows, channels).astype(jnp.bfloat16)
        half = jnp.dot(mixed, mlp_in[layer], preferred_element_type=jnp.float32)
        hidden = (half + half * jnp.tanh(half)).astype(jnp.bfloat16)
        state = state + jnp.dot(
            hidden, mlp_out[layer], preferred_element_type=jnp.float32
        ).reshape(slots * ratio, window_len, channels)
    refined = state.reshape(rows, channels).astype(jnp.bfloat16)
    video = jnp.dot(matrix, refined, preferred_element_type=jnp.float32) / denom
    video_out[...] = video.astype(jnp.bfloat16).reshape(slots, tiles * ratio, channels)
    video_in[me] = video_out[me]
    for there in partners:
        send(video_out.at[there], video_in.at[me], there, video_send, video_recv)

    await_bytes(low_out.at[pl.ds(0, (slots - 1) * pad)], low_send)
    await_bytes(noisy_out.at[pl.ds(0, slots - 1)], noisy_send)
    await_bytes(video_in.at[pl.ds(0, slots - 1)], video_recv)
    video_wide[...] = video_in[...].reshape(video_rows, channels).astype(jnp.float32)
    for t in range(tiles):
        for r in range(ratio):
            out_ref[0, pl.ds(t * tile_pos + r, low_pos, stride=ratio), :] = video_wide[
                pl.ds(t * ratio + r, low_pos, stride=tiles * ratio), :
            ]
    await_bytes(video_out.at[pl.ds(0, slots - 1)], video_send)


def split_on_device(*args):
    (lowres, noisy, starts, blend, assign, base_w, cond_w, noise_w, gains, tconv, mlp_in,
     mlp_out) = args
    slots = assign.shape[0]
    tiles = slots // starts.shape[0]
    _, window_len, tile_pos, channels = noisy.shape
    low_pos = lowres.shape[1] // tiles
    ratio = tile_pos // low_pos
    rows = slots * ratio * window_len
    half, full, whole = jnp.bfloat16, jnp.float32, jnp.int32
    dma = pltpu.SemaphoreType.DMA
    return pl.pallas_call(
        split_kernel,
        out_shape=jax.ShapeDtypeStruct((1, tiles * tile_pos, channels), full),
        in_specs=[pl.BlockSpec(memory_space=pl.ANY)] * len(args),
        out_specs=pl.BlockSpec(memory_space=pltpu.VMEM),
        scratch_shapes=[
            pltpu.VMEM((tiles, low_pos, channels), half),
            pltpu.VMEM(noisy.shape[1:], half),
            pltpu.SMEM(starts.shape, whole),
            pltpu.SMEM(blend.shape, whole),
            pltpu.SMEM(assign.shape, whole),
            pltpu.VMEM(base_w.shape, half),
            pltpu.VMEM(cond_w.shape, half),
            pltpu.VMEM(noise_w.shape, half),
            pltpu.VMEM(gains.shape, full),
            pltpu.VMEM(tconv.shape, full),
            pltpu.VMEM(mlp_in.shape, half),
            pltpu.VMEM(mlp_out.shape, half),
            pltpu.VMEM((slots * SUBLANES, channels), full),
            pltpu.VMEM(((slots + 2) * SUBLANES, channels), full),
            pltpu.VMEM((window_len * tile_pos, channels), full),
            pltpu.VMEM((slots, ratio * window_len, channels), half),
            pltpu.VMEM((slots, ratio * window_len, channels), half),
            pltpu.VMEM((tiles * slots, channels), full),
            pltpu.VMEM((tiles, slots - window_len + 1, window_len, channels), full),
            pltpu.VMEM((slots, 1, window_len, channels), full),
            pltpu.VMEM((slots, tiles * ratio, channels), half),
            pltpu.VMEM((slots, tiles * ratio, channels), half),
            pltpu.VMEM((slots * tiles * ratio, channels), full),
            dma((len(args),)), dma, dma, dma, dma, dma, dma,
        ],
        compiler_params=pltpu.CompilerParams(
            collective_id=0, has_side_effects=True, vmem_limit_bytes=60 * 1024 * 1024
        ),
    )(lowres.reshape(tiles, low_pos, channels), *args[1:]).astype(half)


def on_device(*args):
    lowres, noisy, starts, _, assign = args[:5]
    slots = assign.shape[0]
    tiles = slots // starts.shape[0]
    low_pos = lowres.shape[1] // tiles
    ratio = noisy.shape[2] // low_pos
    if (
        low_pos == slots and tiles <= SUBLANES and noisy.shape[1] == SUBLANES
        and (tiles * ratio) % 16 == 0
    ):
        return split_on_device(*args)
    return slot_on_device(2, *args)


def solution(mesh):
    in_specs = (
        P(("groups", AXIS), None, None),
        P(("groups", AXIS), None, None, None),
        P("groups"),
        P("groups", None),
        P("groups"),
        P(),
        P(),
        P(),
        P(),
        P(),
        P(),
        P(),
    )
    out_specs = P(("groups", AXIS), None, None)
    return jax.shard_map(
        on_device,
        mesh=mesh, in_specs=in_specs, out_specs=out_specs, check_vma=False
    )
```

```python
import functools

import jax
import jax.numpy as jnp
from jax import lax
from jax.experimental import pallas as pl
from jax.experimental.pallas import tpu as pltpu
from jax.sharding import PartitionSpec as P

AXIS = "frame"
UNROLL_UP_TO = 16
SUBLANES = 8


def each(count, body, carry=None):
    if count <= UNROLL_UP_TO:
        for index in range(count):
            carry = body(index, carry)
        return carry
    return lax.fori_loop(0, count, body, carry)


def slot_kernel(
    chunks,
    lowres_hbm, noisy_hbm, starts_hbm, blend_hbm, assign_hbm, base_w_hbm, cond_w_hbm, noise_w_hbm,
    gains_hbm, tconv_hbm, mlp_in_hbm, mlp_out_hbm,
    out_ref,
    lowres, noisy, starts, blend, assign, base_w, cond_w, noise_w, gains, tconv, mlp_in, mlp_out,
    tile_out, tile_in, state_ref, lifted, refined, frames_out, frames_in, weights,
    load_sem, tile_send_sem, tile_recv_sem, frame_send_sem, frame_recv_sem,
):
    slots = assign.shape[0]
    windows, window_len = blend.shape
    tiles = slots // windows
    tile_pos, channels = noisy.shape[1], noisy.shape[2]
    low_pos = lowres.shape[1]
    ratio = tile_pos // low_pos
    layers = gains.shape[0]
    part = tile_pos // chunks
    me = lax.axis_index(AXIS)

    loads = {}
    for spot, (name, source, target) in enumerate((
        ("assign", assign_hbm, assign),
        ("lowres", lowres_hbm, lowres),
        ("starts", starts_hbm, starts),
        ("blend", blend_hbm, blend),
        ("noisy", noisy_hbm.at[0], noisy),
        ("noise_w", noise_w_hbm, noise_w),
        ("base_w", base_w_hbm, base_w),
        ("cond_w", cond_w_hbm, cond_w),
        ("gains", gains_hbm, gains),
        ("tconv", tconv_hbm, tconv),
        ("mlp_in", mlp_in_hbm, mlp_in),
        ("mlp_out", mlp_out_hbm, mlp_out),
    )):
        loads[name] = pltpu.make_async_copy(source, target, load_sem.at[spot])
        loads[name].start()

    def partner(step):
        half = slots // 2
        offset = half + (step + 1) // 2 * (1 - 2 * (step % 2))
        return lax.rem(me + offset + slots, slots)

    barrier = pltpu.get_barrier_semaphore()

    def greet(step, carry):
        pl.semaphore_signal(
            barrier, inc=1, device_id={AXIS: partner(step)}, device_id_type=pl.DeviceIdType.MESH
        )
        return carry

    each(slots - 1, greet)

    zero_tile = jnp.zeros((low_pos, channels), tile_in.dtype)
    tile_in[0] = zero_tile
    tile_in[slots + 1] = zero_tile
    loads["assign"].wait()
    loads["lowres"].wait()

    def tile_for(slot):
        return lowres[lax.rem(assign[slot], tiles)]

    def pick(slot, carry):
        tile_out[slot] = tile_for(slot)
        return carry

    each(slots, pick)
    tile_in[me + 1] = tile_for(me)

    pl.semaphore_wait(barrier, slots - 1)

    def send_tile(step, carry):
        there = partner(step)
        pltpu.make_async_remote_copy(
            src_ref=tile_out.at[there],
            dst_ref=tile_in.at[me + 1],
            send_sem=tile_send_sem,
            recv_sem=tile_recv_sem,
            device_id={AXIS: there},
            device_id_type=pl.DeviceIdType.MESH,
        ).start()
        return carry

    each(slots - 1, send_tile)

    loads["noisy"].wait()
    loads["noise_w"].wait()
    rows = window_len * tile_pos
    state_ref[...] = jnp.dot(
        noisy[...].reshape(rows, channels), noise_w[...], preferred_element_type=jnp.float32
    ).reshape(window_len, tile_pos, channels)

    loads["starts"].wait()
    loads["blend"].wait()

    def weigh(slot, total):
        item = assign[slot]
        window = lax.div(item, tiles)
        tile = lax.rem(item, tiles)
        offset = me - starts[window]
        inside = jnp.logical_and(offset >= 0, offset < window_len)
        value = blend[window, jnp.clip(offset, 0, window_len - 1)]
        value = jnp.where(inside, value, 0)
        for t in range(tiles):
            weights[slot * tiles + t] = jnp.where(tile == t, value, 0).astype(jnp.float32)
        return total + jnp.where(tile == 0, value, 0)

    denom = each(slots, weigh, jnp.int32(0)).astype(jnp.float32)
    start = starts[lax.div(assign[me], tiles)]

    loads["gains"].wait()
    loads["tconv"].wait()
    loads["base_w"].wait()
    loads["cond_w"].wait()
    pltpu.make_async_copy(
        tile_in.at[pl.ds(0, slots - 1)],
        tile_in.at[pl.ds(0, slots - 1)],
        tile_recv_sem,
    ).wait()

    low_rows = window_len * low_pos
    near = [tile_in[start + k] for k in range(window_len + 2)]
    seen = [jnp.concatenate(near[k : k + window_len], 0) for k in range(3)]
    total = jnp.dot(seen[0], base_w[0], preferred_element_type=jnp.float32)
    total = total + jnp.dot(seen[1], base_w[1], preferred_element_type=jnp.float32)
    total = total + jnp.dot(seen[2], base_w[2], preferred_element_type=jnp.float32)
    half = total * 0.5
    base = (seen[1].astype(jnp.float32) + (half + half * jnp.tanh(half))).astype(jnp.bfloat16)
    projected = jnp.dot(base, cond_w[...], preferred_element_type=jnp.float32)
    for r in range(ratio):
        lifted[pl.ds(r, low_rows, stride=ratio), :] = projected

    loads["mlp_in"].wait()
    loads["mlp_out"].wait()
    for c in range(chunks):
        span = pl.ds(c * part, part)
        state = state_ref[:, span, :] + lifted[...].reshape(window_len, tile_pos, channels)[
            :, c * part : (c + 1) * part
        ]
        zeros_frame = jnp.zeros((1, part, channels), jnp.float32)
        for layer in range(layers):
            inverse = lax.rsqrt(jnp.mean(state * state, axis=-1, keepdims=True) + 1e-06)
            plain = state * inverse
            gain = gains[pl.ds(layer, 1), :] * 0.5
            taps = tconv[layer]
            before = (taps[0:1] * gain).reshape(1, 1, channels)
            here = (gain + taps[1:2] * gain).reshape(1, 1, channels)
            behind = (taps[2:3] * gain).reshape(1, 1, channels)
            mixed = (
                here * plain
                + before * jnp.concatenate([zeros_frame, plain[:-1]], 0)
                + behind * jnp.concatenate([plain[1:], zeros_frame], 0)
            )
            mixed = mixed.reshape(window_len * part, channels).astype(jnp.bfloat16)
            half = jnp.dot(mixed, mlp_in[layer], preferred_element_type=jnp.float32)
            hidden = (half + half * jnp.tanh(half)).astype(jnp.bfloat16)
            state = state + jnp.dot(
                hidden, mlp_out[layer], preferred_element_type=jnp.float32
            ).reshape(window_len, part, channels)
        refined[c] = state.astype(jnp.bfloat16)

        def place(frame, carry, c=c):
            frames_out[c, frame] = refined[c, jnp.clip(frame - start, 0, window_len - 1)]
            return carry

        each(slots, place)
        frames_in[c, me] = refined[c, jnp.clip(me - start, 0, window_len - 1)]

        def send_frame(step, carry, c=c):
            there = partner(step)
            pltpu.make_async_remote_copy(
                src_ref=frames_out.at[c, there],
                dst_ref=frames_in.at[c, me],
                send_sem=frame_send_sem.at[c],
                recv_sem=frame_recv_sem.at[c],
                device_id={AXIS: there},
                device_id_type=pl.DeviceIdType.MESH,
            ).start()
            return carry

        each(slots - 1, send_frame)

    scale = jnp.full((1, channels), 1.0, jnp.float32) / jnp.full((1, channels), denom, jnp.float32)
    for c in range(chunks):
        arrived = frames_in.at[c, pl.ds(0, slots - 1)]
        pltpu.make_async_copy(arrived, arrived, frame_recv_sem.at[c]).wait()

        def add(slot, sums, c=c):
            value = frames_in[c, slot].astype(jnp.float32)
            return tuple(
                sums[t] + weights[slot * tiles + t] * value for t in range(tiles)
            )

        sums = each(slots, add, tuple(jnp.zeros((part, channels), jnp.float32) for _ in range(tiles)))
        for t in range(tiles):
            out_ref[0, pl.ds(t * tile_pos + c * part, part), :] = (sums[t] * scale).astype(
                out_ref.dtype
            )

    sent = tile_out.at[pl.ds(0, slots - 1)]
    pltpu.make_async_copy(sent, sent, tile_send_sem).wait()
    for c in range(chunks):
        sent = frames_out.at[c, pl.ds(0, slots - 1)]
        pltpu.make_async_copy(sent, sent, frame_send_sem.at[c]).wait()


def slot_on_device(chunks, *args):
    (lowres, noisy, starts, blend, assign, base_w, cond_w, noise_w, gains, tconv, mlp_in,
     mlp_out) = args
    slots = assign.shape[0]
    windows = starts.shape[0]
    tiles = slots // windows
    _, window_len, tile_pos, channels = noisy.shape
    low_pos = lowres.shape[1] // tiles
    part = tile_pos // chunks
    half = jnp.bfloat16
    full = jnp.float32
    whole = jnp.int32
    return pl.pallas_call(
        functools.partial(slot_kernel, chunks),
        out_shape=jax.ShapeDtypeStruct((1, tiles * tile_pos, channels), half),
        in_specs=[pl.BlockSpec(memory_space=pltpu.HBM)] * len(args),
        out_specs=pl.BlockSpec(memory_space=pltpu.VMEM),
        scratch_shapes=[
            pltpu.VMEM((tiles, low_pos, channels), half),
            pltpu.VMEM(noisy.shape[1:], half),
            pltpu.SMEM(starts.shape, whole),
            pltpu.SMEM(blend.shape, whole),
            pltpu.SMEM(assign.shape, whole),
            pltpu.VMEM(base_w.shape, half),
            pltpu.VMEM(cond_w.shape, half),
            pltpu.VMEM(noise_w.shape, half),
            pltpu.VMEM(gains.shape, full),
            pltpu.VMEM(tconv.shape, full),
            pltpu.VMEM(mlp_in.shape, half),
            pltpu.VMEM(mlp_out.shape, half),
            pltpu.VMEM((slots, low_pos, channels), half),
            pltpu.VMEM((slots + 2, low_pos, channels), half),
            pltpu.VMEM((window_len, tile_pos, channels), full),
            pltpu.VMEM((window_len * tile_pos, channels), full),
            pltpu.VMEM((chunks, window_len, part, channels), half),
            pltpu.VMEM((chunks, slots, part, channels), half),
            pltpu.VMEM((chunks, slots, part, channels), half),
            pltpu.SMEM((slots * tiles,), full),
            pltpu.SemaphoreType.DMA((len(args),)),
            pltpu.SemaphoreType.DMA,
            pltpu.SemaphoreType.DMA,
            pltpu.SemaphoreType.DMA((chunks,)),
            pltpu.SemaphoreType.DMA((chunks,)),
        ],
        compiler_params=pltpu.CompilerParams(
            collective_id=0, has_side_effects=True, vmem_limit_bytes=60 * 1024 * 1024
        ),
    )(lowres.reshape(tiles, low_pos, channels), *args[1:])


def split_kernel(
    lowres_hbm, noisy_hbm, starts_hbm, blend_hbm, assign_hbm, base_w_hbm, cond_w_hbm, noise_w_hbm,
    gains_hbm, tconv_hbm, mlp_in_hbm, mlp_out_hbm,
    out_ref,
    lowres, noisy, starts, blend, assign, base_w, cond_w, noise_w, gains, tconv, mlp_in, mlp_out,
    low_out, low_in, noisy_wide, noisy_out, noisy_in, projected, shifted, cond_ref,
    video_out,
    load_sem, low_send, low_recv, noisy_send, noisy_recv, video_send, video_recv, own_sem,
):
    slots = assign.shape[0]
    windows, window_len = blend.shape
    tiles, low_pos, channels = lowres.shape
    tile_pos = noisy.shape[1]
    ratio = tile_pos // low_pos
    layers = gains.shape[0]
    me = lax.axis_index(AXIS)

    loads = {}
    for spot, (name, source, target) in enumerate((
        ("lowres", lowres_hbm, lowres),
        ("noisy", noisy_hbm.at[0], noisy),
        ("assign", assign_hbm, assign),
        ("starts", starts_hbm, starts),
        ("blend", blend_hbm, blend),
        ("base_w", base_w_hbm, base_w),
        ("cond_w", cond_w_hbm, cond_w),
        ("noise_w", noise_w_hbm, noise_w),
        ("gains", gains_hbm, gains),
        ("tconv", tconv_hbm, tconv),
        ("mlp_in", mlp_in_hbm, mlp_in),
        ("mlp_out", mlp_out_hbm, mlp_out),
    )):
        loads[name] = pltpu.make_async_copy(source, target, load_sem.at[spot])
        loads[name].start()

    partners = []
    for step in range(slots - 1):
        offset = slots // 2 + (step + 1) // 2 * (1 - 2 * (step % 2))
        partners.append(lax.rem(me + offset, slots))

    barrier = pltpu.get_barrier_semaphore()
    for there in partners:
        pl.semaphore_signal(
            barrier, inc=1, device_id={AXIS: there}, device_id_type=pl.DeviceIdType.MESH
        )

    def send(source, target, there, send_sem, recv_sem):
        pltpu.make_async_remote_copy(
            src_ref=source, dst_ref=target, send_sem=send_sem, recv_sem=recv_sem,
            device_id={AXIS: there}, device_id_type=pl.DeviceIdType.MESH,
        ).start()

    def await_bytes(ref, sem):
        pltpu.make_async_copy(ref, ref, sem).wait()

    zero_slab = jnp.zeros((tiles, channels), jnp.float32)
    low_in[0] = zero_slab
    low_in[slots + 1] = zero_slab
    loads["lowres"].wait()
    for t in range(tiles):
        low_out[:, t, :] = lowres[t].astype(jnp.float32)
    low_in[me + 1] = low_out[me]

    loads["noisy"].wait()
    noisy_wide[...] = noisy[...].reshape(window_len * tile_pos, channels).astype(jnp.float32)
    for j in range(slots):
        picked = [
            noisy_wide[pl.ds(j * ratio + r, window_len, stride=tile_pos), :] for r in range(ratio)
        ]
        noisy_out[j] = jnp.concatenate(picked, 0).astype(jnp.bfloat16)
    noisy_in[me] = noisy_out[me]

    pl.semaphore_wait(barrier, slots - 1)
    for there in partners:
        send(low_out.at[there], low_in.at[me + 1], there, low_send, low_recv)
    for there in partners:
        send(noisy_out.at[there], noisy_in.at[me], there, noisy_send, noisy_recv)

    for name in ("assign", "starts", "blend"):
        loads[name].wait()
    rows = slots * ratio * window_len
    lane = lax.broadcasted_iota(jnp.int32, (1, rows), 1)
    lane_slot = lane // (ratio * window_len)
    lane_pos = (lane // window_len) % ratio
    lane_step = lane % window_len
    first = jnp.zeros((1, rows), jnp.int32)
    lane_tile = jnp.zeros((1, rows), jnp.int32)
    lane_window = jnp.zeros((1, rows), jnp.int32)
    for d in range(slots):
        item = assign[d]
        here = lane_slot == d
        window = lax.div(item, tiles)
        lane_window = jnp.where(here, window, lane_window)
        lane_tile = jnp.where(here, lax.rem(item, tiles), lane_tile)
        first = jnp.where(here, starts[window], first)
    factor = jnp.zeros((1, rows), jnp.int32)
    for w in range(windows):
        for k in range(window_len):
            factor = jnp.where(
                jnp.logical_and(lane_window == w, lane_step == k), blend[w, k], factor
            )
    target = ((first + lane_step) * tiles + lane_tile) * ratio + lane_pos
    video_rows = slots * tiles * ratio
    row = lax.broadcasted_iota(jnp.int32, (video_rows, rows), 0)
    matrix = jnp.where(row == target, factor.astype(jnp.float32), 0.0)
    denom = jnp.sum(matrix, axis=1, keepdims=True)
    matrix = matrix.astype(jnp.bfloat16)

    for name in ("base_w", "cond_w", "noise_w", "gains", "tconv"):
        loads[name].wait()
    await_bytes(low_in.at[pl.ds(0, slots - 1)], low_recv)
    total = None
    for k in range(3):
        seen = jnp.concatenate(
            [low_in[k : k + slots, t, :] for t in range(tiles)], 0
        )
        if k == 1:
            centre = seen
        term = jnp.dot(seen.astype(jnp.bfloat16), base_w[k], preferred_element_type=jnp.float32)
        total = term if total is None else total + term
    half = total * 0.5
    base = (centre + (half + half * jnp.tanh(half))).astype(jnp.bfloat16)
    projected[...] = jnp.dot(base, cond_w[...], preferred_element_type=jnp.float32)
    for t in range(tiles):
        for f in range(slots - window_len + 1):
            shifted[t, f] = projected[pl.ds(t * slots + f, window_len), :]
    for d in range(slots):
        item = assign[d]
        cond_ref[d, 0] = shifted[lax.rem(item, tiles), starts[lax.div(item, tiles)]]

    loads["mlp_in"].wait()
    loads["mlp_out"].wait()
    await_bytes(noisy_in.at[pl.ds(0, slots - 1)], noisy_recv)
    state = jnp.dot(
        noisy_in[...].reshape(rows, channels), noise_w[...], preferred_element_type=jnp.float32
    ).reshape(slots, ratio, window_len, channels)
    state = (state + cond_ref[...]).reshape(slots * ratio, window_len, channels)
    step_row = lax.broadcasted_iota(jnp.int32, (window_len, channels), 0)
    for layer in range(layers):
        inverse = lax.rsqrt(jnp.mean(state * state, axis=-1, keepdims=True) + 1e-06)
        plain = state * inverse
        gain = gains[pl.ds(layer, 1), :] * 0.5
        taps = tconv[layer]
        before = jnp.where(step_row == 0, 0.0, taps[0:1] * gain)
        here = gain + taps[1:2] * gain
        behind = jnp.where(step_row == window_len - 1, 0.0, taps[2:3] * gain)
        mixed = (
            here[None] * plain
            + before[None] * pltpu.roll(plain, 1, 1)
            + behind[None] * pltpu.roll(plain, window_len - 1, 1)
        )
        mixed = mixed.reshape(rows, channels).astype(jnp.bfloat16)
        half = jnp.dot(mixed, mlp_in[layer], preferred_element_type=jnp.float32)
        hidden = (half + half * jnp.tanh(half)).astype(jnp.bfloat16)
        state = state + jnp.dot(
            hidden, mlp_out[layer], preferred_element_type=jnp.float32
        ).reshape(slots * ratio, window_len, channels)
    refined = state.reshape(rows, channels).astype(jnp.bfloat16)
    video = jnp.dot(matrix, refined, preferred_element_type=jnp.float32) / denom
    video_out[...] = video.astype(jnp.bfloat16).reshape(slots, tiles * ratio, channels)
    for there in partners:
        send(video_out.at[there], out_ref.at[me], there, video_send, video_recv)
    own = pltpu.make_async_copy(video_out.at[me], out_ref.at[me], own_sem)
    own.start()

    await_bytes(low_out.at[pl.ds(0, slots - 1)], low_send)
    await_bytes(noisy_out.at[pl.ds(0, slots - 1)], noisy_send)
    await_bytes(out_ref.at[pl.ds(0, slots - 1)], video_recv)
    own.wait()
    await_bytes(video_out.at[pl.ds(0, slots - 1)], video_send)


def order_kernel(tiles, video_ref, out_ref, wide, ordered):
    sources, rows, channels = video_ref.shape
    ratio = rows // tiles
    tile_pos = sources * ratio
    wide[...] = video_ref[...].reshape(sources * rows, channels).astype(jnp.float32)
    for t in range(tiles):
        for r in range(ratio):
            ordered[pl.ds(t * tile_pos + r, sources, stride=ratio), :] = wide[
                pl.ds(t * ratio + r, sources, stride=rows), :
            ]
    out_ref[0] = ordered[...].astype(out_ref.dtype)


def split_on_device(*args):
    (lowres, noisy, starts, blend, assign, base_w, cond_w, noise_w, gains, tconv, mlp_in,
     mlp_out) = args
    slots = assign.shape[0]
    tiles = slots // starts.shape[0]
    _, window_len, tile_pos, channels = noisy.shape
    low_pos = lowres.shape[1] // tiles
    ratio = tile_pos // low_pos
    rows = slots * ratio * window_len
    half, full, whole = jnp.bfloat16, jnp.float32, jnp.int32
    dma = pltpu.SemaphoreType.DMA
    video = pl.pallas_call(
        split_kernel,
        out_shape=jax.ShapeDtypeStruct((slots, tiles * ratio, channels), half),
        in_specs=[pl.BlockSpec(memory_space=pl.ANY)] * len(args),
        out_specs=pl.BlockSpec(memory_space=pl.ANY),
        scratch_shapes=[
            pltpu.VMEM((tiles, low_pos, channels), half),
            pltpu.VMEM(noisy.shape[1:], half),
            pltpu.SMEM(starts.shape, whole),
            pltpu.SMEM(blend.shape, whole),
            pltpu.SMEM(assign.shape, whole),
            pltpu.VMEM(base_w.shape, half),
            pltpu.VMEM(cond_w.shape, half),
            pltpu.VMEM(noise_w.shape, half),
            pltpu.VMEM(gains.shape, full),
            pltpu.VMEM(tconv.shape, full),
            pltpu.VMEM(mlp_in.shape, half),
            pltpu.VMEM(mlp_out.shape, half),
            pltpu.VMEM((slots, tiles, channels), full),
            pltpu.VMEM((slots + 2, tiles, channels), full),
            pltpu.VMEM((window_len * tile_pos, channels), full),
            pltpu.VMEM((slots, ratio * window_len, channels), half),
            pltpu.VMEM((slots, ratio * window_len, channels), half),
            pltpu.VMEM((tiles * slots, channels), full),
            pltpu.VMEM((tiles, slots - window_len + 1, window_len, channels), full),
            pltpu.VMEM((slots, 1, window_len, channels), full),
            pltpu.VMEM((slots, tiles * ratio, channels), half),
            dma((len(args),)), dma, dma, dma, dma, dma, dma, dma,
        ],
        compiler_params=pltpu.CompilerParams(
            collective_id=0, has_side_effects=True, vmem_limit_bytes=60 * 1024 * 1024
        ),
    )(lowres.reshape(tiles, low_pos, channels), *args[1:])
    return pl.pallas_call(
        functools.partial(order_kernel, tiles),
        out_shape=jax.ShapeDtypeStruct((1, tiles * tile_pos, channels), half),
        in_specs=[pl.BlockSpec(memory_space=pltpu.VMEM)],
        out_specs=pl.BlockSpec(memory_space=pltpu.VMEM),
        scratch_shapes=[
            pltpu.VMEM((tiles * tile_pos, channels), full),
            pltpu.VMEM((tiles * tile_pos, channels), full),
        ],
        compiler_params=pltpu.CompilerParams(vmem_limit_bytes=60 * 1024 * 1024),
    )(video)


def on_device(*args):
    lowres, noisy, starts, _, assign = args[:5]
    slots = assign.shape[0]
    tiles = slots // starts.shape[0]
    low_pos = lowres.shape[1] // tiles
    ratio = noisy.shape[2] // low_pos
    if (
        low_pos == slots and tiles <= SUBLANES and noisy.shape[1] == SUBLANES
        and (tiles * ratio) % 16 == 0
    ):
        return split_on_device(*args)
    return slot_on_device(2, *args)


def solution(mesh):
    in_specs = (
        P(("groups", AXIS), None, None),
        P(("groups", AXIS), None, None, None),
        P("groups"),
        P("groups", None),
        P("groups"),
        P(),
        P(),
        P(),
        P(),
        P(),
        P(),
        P(),
    )
    out_specs = P(("groups", AXIS), None, None)
    return jax.shard_map(
        on_device,
        mesh=mesh, in_specs=in_specs, out_specs=out_specs, check_vma=False
    )
```

```python
import functools

import jax
import jax.numpy as jnp
from jax import lax
from jax.experimental import pallas as pl
from jax.experimental.pallas import tpu as pltpu
from jax.sharding import PartitionSpec as P

AXIS = "frame"
UNROLL_UP_TO = 16
SUBLANES = 8


def each(count, body, carry=None):
    if count <= UNROLL_UP_TO:
        for index in range(count):
            carry = body(index, carry)
        return carry
    return lax.fori_loop(0, count, body, carry)


def slot_kernel(
    chunks,
    lowres_hbm, noisy_hbm, starts_hbm, blend_hbm, assign_hbm, base_w_hbm, cond_w_hbm, noise_w_hbm,
    gains_hbm, tconv_hbm, mlp_in_hbm, mlp_out_hbm,
    out_ref,
    lowres, noisy, starts, blend, assign, base_w, cond_w, noise_w, gains, tconv, mlp_in, mlp_out,
    tile_out, tile_in, state_ref, lifted, refined, frames_out, frames_in, weights,
    load_sem, tile_send_sem, tile_recv_sem, frame_send_sem, frame_recv_sem,
):
    slots = assign.shape[0]
    windows, window_len = blend.shape
    tiles = slots // windows
    tile_pos, channels = noisy.shape[1], noisy.shape[2]
    low_pos = lowres.shape[1]
    ratio = tile_pos // low_pos
    layers = gains.shape[0]
    part = tile_pos // chunks
    me = lax.axis_index(AXIS)

    loads = {}
    for spot, (name, source, target) in enumerate((
        ("assign", assign_hbm, assign),
        ("lowres", lowres_hbm, lowres),
        ("starts", starts_hbm, starts),
        ("blend", blend_hbm, blend),
        ("noisy", noisy_hbm.at[0], noisy),
        ("noise_w", noise_w_hbm, noise_w),
        ("base_w", base_w_hbm, base_w),
        ("cond_w", cond_w_hbm, cond_w),
        ("gains", gains_hbm, gains),
        ("tconv", tconv_hbm, tconv),
        ("mlp_in", mlp_in_hbm, mlp_in),
        ("mlp_out", mlp_out_hbm, mlp_out),
    )):
        loads[name] = pltpu.make_async_copy(source, target, load_sem.at[spot])
        loads[name].start()

    def partner(step):
        half = slots // 2
        offset = half + (step + 1) // 2 * (1 - 2 * (step % 2))
        return lax.rem(me + offset + slots, slots)

    barrier = pltpu.get_barrier_semaphore()

    def greet(step, carry):
        pl.semaphore_signal(
            barrier, inc=1, device_id={AXIS: partner(step)}, device_id_type=pl.DeviceIdType.MESH
        )
        return carry

    each(slots - 1, greet)

    zero_tile = jnp.zeros((low_pos, channels), tile_in.dtype)
    tile_in[0] = zero_tile
    tile_in[slots + 1] = zero_tile
    loads["assign"].wait()
    loads["lowres"].wait()

    def tile_for(slot):
        return lowres[lax.rem(assign[slot], tiles)]

    def pick(slot, carry):
        tile_out[slot] = tile_for(slot)
        return carry

    each(slots, pick)
    tile_in[me + 1] = tile_for(me)

    pl.semaphore_wait(barrier, slots - 1)

    def send_tile(step, carry):
        there = partner(step)
        pltpu.make_async_remote_copy(
            src_ref=tile_out.at[there],
            dst_ref=tile_in.at[me + 1],
            send_sem=tile_send_sem,
            recv_sem=tile_recv_sem,
            device_id={AXIS: there},
            device_id_type=pl.DeviceIdType.MESH,
        ).start()
        return carry

    each(slots - 1, send_tile)

    loads["noisy"].wait()
    loads["noise_w"].wait()
    rows = window_len * tile_pos
    state_ref[...] = jnp.dot(
        noisy[...].reshape(rows, channels), noise_w[...], preferred_element_type=jnp.float32
    ).reshape(window_len, tile_pos, channels)

    loads["starts"].wait()
    loads["blend"].wait()

    def weigh(slot, total):
        item = assign[slot]
        window = lax.div(item, tiles)
        tile = lax.rem(item, tiles)
        offset = me - starts[window]
        inside = jnp.logical_and(offset >= 0, offset < window_len)
        value = blend[window, jnp.clip(offset, 0, window_len - 1)]
        value = jnp.where(inside, value, 0)
        for t in range(tiles):
            weights[slot * tiles + t] = jnp.where(tile == t, value, 0).astype(jnp.float32)
        return total + jnp.where(tile == 0, value, 0)

    denom = each(slots, weigh, jnp.int32(0)).astype(jnp.float32)
    start = starts[lax.div(assign[me], tiles)]

    loads["gains"].wait()
    loads["tconv"].wait()
    loads["base_w"].wait()
    loads["cond_w"].wait()
    pltpu.make_async_copy(
        tile_in.at[pl.ds(0, slots - 1)],
        tile_in.at[pl.ds(0, slots - 1)],
        tile_recv_sem,
    ).wait()

    low_rows = window_len * low_pos
    near = [tile_in[start + k] for k in range(window_len + 2)]
    seen = [jnp.concatenate(near[k : k + window_len], 0) for k in range(3)]
    total = jnp.dot(seen[0], base_w[0], preferred_element_type=jnp.float32)
    total = total + jnp.dot(seen[1], base_w[1], preferred_element_type=jnp.float32)
    total = total + jnp.dot(seen[2], base_w[2], preferred_element_type=jnp.float32)
    half = total * 0.5
    base = (seen[1].astype(jnp.float32) + (half + half * jnp.tanh(half))).astype(jnp.bfloat16)
    projected = jnp.dot(base, cond_w[...], preferred_element_type=jnp.float32)
    for r in range(ratio):
        lifted[pl.ds(r, low_rows, stride=ratio), :] = projected

    loads["mlp_in"].wait()
    loads["mlp_out"].wait()
    for c in range(chunks):
        span = pl.ds(c * part, part)
        state = state_ref[:, span, :] + lifted[...].reshape(window_len, tile_pos, channels)[
            :, c * part : (c + 1) * part
        ]
        zeros_frame = jnp.zeros((1, part, channels), jnp.float32)
        for layer in range(layers):
            inverse = lax.rsqrt(jnp.mean(state * state, axis=-1, keepdims=True) + 1e-06)
            plain = state * inverse
            gain = gains[pl.ds(layer, 1), :] * 0.5
            taps = tconv[layer]
            before = (taps[0:1] * gain).reshape(1, 1, channels)
            here = (gain + taps[1:2] * gain).reshape(1, 1, channels)
            behind = (taps[2:3] * gain).reshape(1, 1, channels)
            mixed = (
                here * plain
                + before * jnp.concatenate([zeros_frame, plain[:-1]], 0)
                + behind * jnp.concatenate([plain[1:], zeros_frame], 0)
            )
            mixed = mixed.reshape(window_len * part, channels).astype(jnp.bfloat16)
            half = jnp.dot(mixed, mlp_in[layer], preferred_element_type=jnp.float32)
            hidden = (half + half * jnp.tanh(half)).astype(jnp.bfloat16)
            state = state + jnp.dot(
                hidden, mlp_out[layer], preferred_element_type=jnp.float32
            ).reshape(window_len, part, channels)
        refined[c] = state.astype(jnp.bfloat16)

        def place(frame, carry, c=c):
            frames_out[c, frame] = refined[c, jnp.clip(frame - start, 0, window_len - 1)]
            return carry

        each(slots, place)
        frames_in[c, me] = refined[c, jnp.clip(me - start, 0, window_len - 1)]

        def send_frame(step, carry, c=c):
            there = partner(step)
            pltpu.make_async_remote_copy(
                src_ref=frames_out.at[c, there],
                dst_ref=frames_in.at[c, me],
                send_sem=frame_send_sem.at[c],
                recv_sem=frame_recv_sem.at[c],
                device_id={AXIS: there},
                device_id_type=pl.DeviceIdType.MESH,
            ).start()
            return carry

        each(slots - 1, send_frame)

    scale = jnp.full((1, channels), 1.0, jnp.float32) / jnp.full((1, channels), denom, jnp.float32)
    for c in range(chunks):
        arrived = frames_in.at[c, pl.ds(0, slots - 1)]
        pltpu.make_async_copy(arrived, arrived, frame_recv_sem.at[c]).wait()

        def add(slot, sums, c=c):
            value = frames_in[c, slot].astype(jnp.float32)
            return tuple(
                sums[t] + weights[slot * tiles + t] * value for t in range(tiles)
            )

        sums = each(slots, add, tuple(jnp.zeros((part, channels), jnp.float32) for _ in range(tiles)))
        for t in range(tiles):
            out_ref[0, pl.ds(t * tile_pos + c * part, part), :] = (sums[t] * scale).astype(
                out_ref.dtype
            )

    sent = tile_out.at[pl.ds(0, slots - 1)]
    pltpu.make_async_copy(sent, sent, tile_send_sem).wait()
    for c in range(chunks):
        sent = frames_out.at[c, pl.ds(0, slots - 1)]
        pltpu.make_async_copy(sent, sent, frame_send_sem.at[c]).wait()


def slot_on_device(chunks, *args):
    (lowres, noisy, starts, blend, assign, base_w, cond_w, noise_w, gains, tconv, mlp_in,
     mlp_out) = args
    slots = assign.shape[0]
    windows = starts.shape[0]
    tiles = slots // windows
    _, window_len, tile_pos, channels = noisy.shape
    low_pos = lowres.shape[1] // tiles
    part = tile_pos // chunks
    half = jnp.bfloat16
    full = jnp.float32
    whole = jnp.int32
    return pl.pallas_call(
        functools.partial(slot_kernel, chunks),
        out_shape=jax.ShapeDtypeStruct((1, tiles * tile_pos, channels), half),
        in_specs=[pl.BlockSpec(memory_space=pltpu.HBM)] * len(args),
        out_specs=pl.BlockSpec(memory_space=pltpu.VMEM),
        scratch_shapes=[
            pltpu.VMEM((tiles, low_pos, channels), half),
            pltpu.VMEM(noisy.shape[1:], half),
            pltpu.SMEM(starts.shape, whole),
            pltpu.SMEM(blend.shape, whole),
            pltpu.SMEM(assign.shape, whole),
            pltpu.VMEM(base_w.shape, half),
            pltpu.VMEM(cond_w.shape, half),
            pltpu.VMEM(noise_w.shape, half),
            pltpu.VMEM(gains.shape, full),
            pltpu.VMEM(tconv.shape, full),
            pltpu.VMEM(mlp_in.shape, half),
            pltpu.VMEM(mlp_out.shape, half),
            pltpu.VMEM((slots, low_pos, channels), half),
            pltpu.VMEM((slots + 2, low_pos, channels), half),
            pltpu.VMEM((window_len, tile_pos, channels), full),
            pltpu.VMEM((window_len * tile_pos, channels), full),
            pltpu.VMEM((chunks, window_len, part, channels), half),
            pltpu.VMEM((chunks, slots, part, channels), half),
            pltpu.VMEM((chunks, slots, part, channels), half),
            pltpu.SMEM((slots * tiles,), full),
            pltpu.SemaphoreType.DMA((len(args),)),
            pltpu.SemaphoreType.DMA,
            pltpu.SemaphoreType.DMA,
            pltpu.SemaphoreType.DMA((chunks,)),
            pltpu.SemaphoreType.DMA((chunks,)),
        ],
        compiler_params=pltpu.CompilerParams(
            collective_id=0, has_side_effects=True, vmem_limit_bytes=60 * 1024 * 1024
        ),
    )(lowres.reshape(tiles, low_pos, channels), *args[1:])


def split_kernel(
    lowres_hbm, noisy_hbm, starts_hbm, blend_hbm, assign_hbm, base_w_hbm, cond_w_hbm, noise_w_hbm,
    gains_hbm, tconv_hbm, mlp_in_hbm, mlp_out_hbm,
    out_ref,
    lowres, noisy, starts, blend, assign, base_w, cond_w, noise_w, gains, tconv, mlp_in, mlp_out,
    low_out, low_in, noisy_wide, noisy_out, noisy_in, projected, shifted, cond_ref,
    video_out, matrices,
    load_sem, low_send, low_recv, noisy_send, noisy_recv, video_send, video_recv, own_sem,
):
    slots = assign.shape[0]
    windows, window_len = blend.shape
    tiles, low_pos, channels = lowres.shape
    tile_pos = noisy.shape[1]
    ratio = tile_pos // low_pos
    layers = gains.shape[0]
    me = lax.axis_index(AXIS)

    loads = {}
    for spot, (name, source, target) in enumerate((
        ("lowres", lowres_hbm, lowres),
        ("noisy", noisy_hbm.at[0], noisy),
        ("assign", assign_hbm, assign),
        ("starts", starts_hbm, starts),
        ("blend", blend_hbm, blend),
        ("base_w", base_w_hbm, base_w),
        ("cond_w", cond_w_hbm, cond_w),
        ("noise_w", noise_w_hbm, noise_w),
        ("gains", gains_hbm, gains),
        ("tconv", tconv_hbm, tconv),
        ("mlp_in", mlp_in_hbm, mlp_in),
        ("mlp_out", mlp_out_hbm, mlp_out),
    )):
        loads[name] = pltpu.make_async_copy(source, target, load_sem.at[spot])
        loads[name].start()

    half_slots = slots // 2
    side, place = me // half_slots, me % half_slots
    away = [
        (1 - side) * half_slots + lax.rem(place + step, half_slots) for step in range(half_slots)
    ]
    near = [
        side * half_slots + lax.rem(place + step, half_slots) for step in range(1, half_slots)
    ]
    partners = away + near

    barrier = pltpu.get_barrier_semaphore()
    for there in partners:
        pl.semaphore_signal(
            barrier, inc=1, device_id={AXIS: there}, device_id_type=pl.DeviceIdType.MESH
        )

    def send(source, target, there, send_sem, recv_sem):
        pltpu.make_async_remote_copy(
            src_ref=source, dst_ref=target, send_sem=send_sem, recv_sem=recv_sem,
            device_id={AXIS: there}, device_id_type=pl.DeviceIdType.MESH,
        ).start()

    def await_bytes(ref, sem):
        pltpu.make_async_copy(ref, ref, sem).wait()

    zero_slab = jnp.zeros((tiles, channels), jnp.float32)
    low_in[0] = zero_slab
    low_in[slots + 1] = zero_slab
    loads["lowres"].wait()
    for t in range(tiles):
        low_out[:, t, :] = lowres[t].astype(jnp.float32)
    low_in[me + 1] = low_out[me]

    loads["noisy"].wait()
    noisy_wide[...] = noisy[...].reshape(window_len * tile_pos, channels).astype(jnp.float32)
    for j in range(slots):
        picked = [
            noisy_wide[pl.ds(j * ratio + r, window_len, stride=tile_pos), :] for r in range(ratio)
        ]
        noisy_out[j] = jnp.concatenate(picked, 0).astype(jnp.bfloat16)
    noisy_in[side, place] = noisy_out[me]

    pl.semaphore_wait(barrier, slots - 1)
    for there in partners:
        send(low_out.at[there], low_in.at[me + 1], there, low_send, low_recv)
    for group, targets in enumerate((near, away)):
        for there in targets:
            send(
                noisy_out.at[there], noisy_in.at[side, place], there,
                noisy_send, noisy_recv.at[group],
            )

    for name in ("assign", "starts", "blend"):
        loads[name].wait()
    rows = slots * ratio * window_len
    lane = lax.broadcasted_iota(jnp.int32, (1, rows), 1)
    lane_slot = lane // (ratio * window_len)
    lane_pos = (lane // window_len) % ratio
    lane_step = lane % window_len
    first = jnp.zeros((1, rows), jnp.int32)
    lane_tile = jnp.zeros((1, rows), jnp.int32)
    lane_window = jnp.zeros((1, rows), jnp.int32)
    for d in range(slots):
        item = assign[d]
        here = lane_slot == d
        window = lax.div(item, tiles)
        lane_window = jnp.where(here, window, lane_window)
        lane_tile = jnp.where(here, lax.rem(item, tiles), lane_tile)
        first = jnp.where(here, starts[window], first)
    factor = jnp.zeros((1, rows), jnp.int32)
    for w in range(windows):
        for k in range(window_len):
            factor = jnp.where(
                jnp.logical_and(lane_window == w, lane_step == k), blend[w, k], factor
            )
    target = ((first + lane_step) * tiles + lane_tile) * ratio + lane_pos
    video_rows = slots * tiles * ratio
    row = lax.broadcasted_iota(jnp.int32, (video_rows, rows), 0)
    matrix = jnp.where(row == target, factor.astype(jnp.float32), 0.0)
    denom = jnp.sum(matrix, axis=1, keepdims=True)
    scale = 1.0 / denom
    half_rows = rows // 2
    for h in range(2):
        matrices[h] = matrix[:, h * half_rows : (h + 1) * half_rows].astype(jnp.bfloat16)

    for name in ("base_w", "cond_w", "noise_w", "gains", "tconv"):
        loads[name].wait()
    await_bytes(low_in.at[pl.ds(0, slots - 1)], low_recv)
    total = None
    for k in range(3):
        seen = jnp.concatenate(
            [low_in[k : k + slots, t, :] for t in range(tiles)], 0
        )
        if k == 1:
            centre = seen
        term = jnp.dot(seen.astype(jnp.bfloat16), base_w[k], preferred_element_type=jnp.float32)
        total = term if total is None else total + term
    half = total * 0.5
    base = (centre + (half + half * jnp.tanh(half))).astype(jnp.bfloat16)
    projected[...] = jnp.dot(base, cond_w[...], preferred_element_type=jnp.float32)
    for t in range(tiles):
        for f in range(slots - window_len + 1):
            shifted[t, f] = projected[pl.ds(t * slots + f, window_len), :]
    for d in range(slots):
        item = assign[d]
        cond_ref[d // half_slots, d % half_slots, 0] = shifted[lax.rem(item, tiles), starts[lax.div(item, tiles)]]

    loads["mlp_in"].wait()
    loads["mlp_out"].wait()
    step_row = lax.broadcasted_iota(jnp.int32, (window_len, channels), 0)
    groups = half_slots * ratio
    video = None
    for group, chosen in enumerate((side, 1 - side)):
        await_bytes(noisy_in.at[0, pl.ds(0, half_slots - 1 + group)], noisy_recv.at[group])
        state = jnp.dot(
            noisy_in[chosen].reshape(half_rows, channels), noise_w[...],
            preferred_element_type=jnp.float32,
        ).reshape(half_slots, ratio, window_len, channels)
        state = (state + cond_ref[chosen]).reshape(groups, window_len, channels)
        for layer in range(layers):
            inverse = lax.rsqrt(jnp.mean(state * state, axis=-1, keepdims=True) + 1e-06)
            plain = state * inverse
            gain = gains[pl.ds(layer, 1), :] * 0.5
            taps = tconv[layer]
            before = jnp.where(step_row == 0, 0.0, taps[0:1] * gain)
            here = gain + taps[1:2] * gain
            behind = jnp.where(step_row == window_len - 1, 0.0, taps[2:3] * gain)
            mixed = (
                here[None] * plain
                + before[None] * pltpu.roll(plain, 1, 1)
                + behind[None] * pltpu.roll(plain, window_len - 1, 1)
            )
            mixed = mixed.reshape(half_rows, channels).astype(jnp.bfloat16)
            half = jnp.dot(mixed, mlp_in[layer], preferred_element_type=jnp.float32)
            hidden = (half + half * jnp.tanh(half)).astype(jnp.bfloat16)
            state = state + jnp.dot(
                hidden, mlp_out[layer], preferred_element_type=jnp.float32
            ).reshape(groups, window_len, channels)
        refined = state.reshape(half_rows, channels).astype(jnp.bfloat16)
        term = jnp.dot(matrices[chosen], refined, preferred_element_type=jnp.float32)
        video = term if video is None else video + term
    video = video * scale
    video_out[...] = video.astype(jnp.bfloat16).reshape(slots, tiles * ratio, channels)
    for there in partners:
        send(video_out.at[there], out_ref.at[me], there, video_send, video_recv)
    own = pltpu.make_async_copy(video_out.at[me], out_ref.at[me], own_sem)
    own.start()

    await_bytes(low_out.at[pl.ds(0, slots - 1)], low_send)
    await_bytes(noisy_out.at[pl.ds(0, slots - 1)], noisy_send)
    await_bytes(out_ref.at[pl.ds(0, slots - 1)], video_recv)
    own.wait()
    await_bytes(video_out.at[pl.ds(0, slots - 1)], video_send)


def order_kernel(tiles, video_ref, out_ref, wide, ordered):
    sources, rows, channels = video_ref.shape
    ratio = rows // tiles
    tile_pos = sources * ratio
    wide[...] = video_ref[...].reshape(sources * rows, channels).astype(jnp.float32)
    for t in range(tiles):
        for r in range(ratio):
            ordered[pl.ds(t * tile_pos + r, sources, stride=ratio), :] = wide[
                pl.ds(t * ratio + r, sources, stride=rows), :
            ]
    out_ref[0] = ordered[...].astype(out_ref.dtype)


def split_on_device(*args):
    (lowres, noisy, starts, blend, assign, base_w, cond_w, noise_w, gains, tconv, mlp_in,
     mlp_out) = args
    slots = assign.shape[0]
    tiles = slots // starts.shape[0]
    _, window_len, tile_pos, channels = noisy.shape
    low_pos = lowres.shape[1] // tiles
    ratio = tile_pos // low_pos
    rows = slots * ratio * window_len
    half, full, whole = jnp.bfloat16, jnp.float32, jnp.int32
    dma = pltpu.SemaphoreType.DMA
    video = pl.pallas_call(
        split_kernel,
        out_shape=jax.ShapeDtypeStruct((slots, tiles * ratio, channels), half),
        in_specs=[pl.BlockSpec(memory_space=pl.ANY)] * len(args),
        out_specs=pl.BlockSpec(memory_space=pl.ANY),
        scratch_shapes=[
            pltpu.VMEM((tiles, low_pos, channels), half),
            pltpu.VMEM(noisy.shape[1:], half),
            pltpu.SMEM(starts.shape, whole),
            pltpu.SMEM(blend.shape, whole),
            pltpu.SMEM(assign.shape, whole),
            pltpu.VMEM(base_w.shape, half),
            pltpu.VMEM(cond_w.shape, half),
            pltpu.VMEM(noise_w.shape, half),
            pltpu.VMEM(gains.shape, full),
            pltpu.VMEM(tconv.shape, full),
            pltpu.VMEM(mlp_in.shape, half),
            pltpu.VMEM(mlp_out.shape, half),
            pltpu.VMEM((slots, tiles, channels), full),
            pltpu.VMEM((slots + 2, tiles, channels), full),
            pltpu.VMEM((window_len * tile_pos, channels), full),
            pltpu.VMEM((slots, ratio * window_len, channels), half),
            pltpu.VMEM((2, slots // 2, ratio * window_len, channels), half),
            pltpu.VMEM((tiles * slots, channels), full),
            pltpu.VMEM((tiles, slots - window_len + 1, window_len, channels), full),
            pltpu.VMEM((2, slots // 2, 1, window_len, channels), full),
            pltpu.VMEM((slots, tiles * ratio, channels), half),
            pltpu.VMEM((2, slots * tiles * ratio, rows // 2), half),
            dma((len(args),)), dma, dma, dma, dma((2,)), dma, dma, dma,
        ],
        compiler_params=pltpu.CompilerParams(
            collective_id=0, has_side_effects=True, vmem_limit_bytes=60 * 1024 * 1024
        ),
    )(lowres.reshape(tiles, low_pos, channels), *args[1:])
    return pl.pallas_call(
        functools.partial(order_kernel, tiles),
        out_shape=jax.ShapeDtypeStruct((1, tiles * tile_pos, channels), half),
        in_specs=[pl.BlockSpec(memory_space=pltpu.VMEM)],
        out_specs=pl.BlockSpec(memory_space=pltpu.VMEM),
        scratch_shapes=[
            pltpu.VMEM((tiles * tile_pos, channels), full),
            pltpu.VMEM((tiles * tile_pos, channels), full),
        ],
        compiler_params=pltpu.CompilerParams(vmem_limit_bytes=60 * 1024 * 1024),
    )(video)


def on_device(*args):
    lowres, noisy, starts, _, assign = args[:5]
    slots = assign.shape[0]
    tiles = slots // starts.shape[0]
    low_pos = lowres.shape[1] // tiles
    ratio = noisy.shape[2] // low_pos
    if (
        low_pos == slots and slots % 2 == 0 and tiles <= SUBLANES and noisy.shape[1] == SUBLANES
        and (tiles * ratio) % 16 == 0
    ):
        return split_on_device(*args)
    return slot_on_device(2, *args)


def solution(mesh):
    in_specs = (
        P(("groups", AXIS), None, None),
        P(("groups", AXIS), None, None, None),
        P("groups"),
        P("groups", None),
        P("groups"),
        P(),
        P(),
        P(),
        P(),
        P(),
        P(),
        P(),
    )
    out_specs = P(("groups", AXIS), None, None)
    return jax.shard_map(
        on_device,
        mesh=mesh, in_specs=in_specs, out_specs=out_specs, check_vma=False
    )
```

```python
import functools

import jax
import jax.numpy as jnp
from jax import lax
from jax.experimental import pallas as pl
from jax.experimental.pallas import tpu as pltpu
from jax.sharding import PartitionSpec as P

AXIS = "frame"
UNROLL_UP_TO = 16
SUBLANES = 8


def each(count, body, carry=None):
    if count <= UNROLL_UP_TO:
        for index in range(count):
            carry = body(index, carry)
        return carry
    return lax.fori_loop(0, count, body, carry)


def slot_kernel(
    chunks,
    lowres_hbm, noisy_hbm, starts_hbm, blend_hbm, assign_hbm, base_w_hbm, cond_w_hbm, noise_w_hbm,
    gains_hbm, tconv_hbm, mlp_in_hbm, mlp_out_hbm,
    out_ref,
    lowres, noisy, starts, blend, assign, base_w, cond_w, noise_w, gains, tconv, mlp_in, mlp_out,
    tile_out, tile_in, state_ref, lifted, refined, frames_out, frames_in, weights,
    load_sem, tile_send_sem, tile_recv_sem, frame_send_sem, frame_recv_sem,
):
    slots = assign.shape[0]
    windows, window_len = blend.shape
    tiles = slots // windows
    tile_pos, channels = noisy.shape[1], noisy.shape[2]
    low_pos = lowres.shape[1]
    ratio = tile_pos // low_pos
    layers = gains.shape[0]
    part = tile_pos // chunks
    me = lax.axis_index(AXIS)

    loads = {}
    for spot, (name, source, target) in enumerate((
        ("assign", assign_hbm, assign),
        ("lowres", lowres_hbm, lowres),
        ("starts", starts_hbm, starts),
        ("blend", blend_hbm, blend),
        ("noisy", noisy_hbm.at[0], noisy),
        ("noise_w", noise_w_hbm, noise_w),
        ("base_w", base_w_hbm, base_w),
        ("cond_w", cond_w_hbm, cond_w),
        ("gains", gains_hbm, gains),
        ("tconv", tconv_hbm, tconv),
        ("mlp_in", mlp_in_hbm, mlp_in),
        ("mlp_out", mlp_out_hbm, mlp_out),
    )):
        loads[name] = pltpu.make_async_copy(source, target, load_sem.at[spot])
        loads[name].start()

    def partner(step):
        half = slots // 2
        offset = half + (step + 1) // 2 * (1 - 2 * (step % 2))
        return lax.rem(me + offset + slots, slots)

    barrier = pltpu.get_barrier_semaphore()

    def greet(step, carry):
        pl.semaphore_signal(
            barrier, inc=1, device_id={AXIS: partner(step)}, device_id_type=pl.DeviceIdType.MESH
        )
        return carry

    each(slots - 1, greet)

    zero_tile = jnp.zeros((low_pos, channels), tile_in.dtype)
    tile_in[0] = zero_tile
    tile_in[slots + 1] = zero_tile
    loads["assign"].wait()
    loads["lowres"].wait()

    def tile_for(slot):
        return lowres[lax.rem(assign[slot], tiles)]

    def pick(slot, carry):
        tile_out[slot] = tile_for(slot)
        return carry

    each(slots, pick)
    tile_in[me + 1] = tile_for(me)

    pl.semaphore_wait(barrier, slots - 1)

    def send_tile(step, carry):
        there = partner(step)
        pltpu.make_async_remote_copy(
            src_ref=tile_out.at[there],
            dst_ref=tile_in.at[me + 1],
            send_sem=tile_send_sem,
            recv_sem=tile_recv_sem,
            device_id={AXIS: there},
            device_id_type=pl.DeviceIdType.MESH,
        ).start()
        return carry

    each(slots - 1, send_tile)

    loads["noisy"].wait()
    loads["noise_w"].wait()
    rows = window_len * tile_pos
    state_ref[...] = jnp.dot(
        noisy[...].reshape(rows, channels), noise_w[...], preferred_element_type=jnp.float32
    ).reshape(window_len, tile_pos, channels)

    loads["starts"].wait()
    loads["blend"].wait()

    def weigh(slot, total):
        item = assign[slot]
        window = lax.div(item, tiles)
        tile = lax.rem(item, tiles)
        offset = me - starts[window]
        inside = jnp.logical_and(offset >= 0, offset < window_len)
        value = blend[window, jnp.clip(offset, 0, window_len - 1)]
        value = jnp.where(inside, value, 0)
        for t in range(tiles):
            weights[slot * tiles + t] = jnp.where(tile == t, value, 0).astype(jnp.float32)
        return total + jnp.where(tile == 0, value, 0)

    denom = each(slots, weigh, jnp.int32(0)).astype(jnp.float32)
    start = starts[lax.div(assign[me], tiles)]

    loads["gains"].wait()
    loads["tconv"].wait()
    loads["base_w"].wait()
    loads["cond_w"].wait()
    pltpu.make_async_copy(
        tile_in.at[pl.ds(0, slots - 1)],
        tile_in.at[pl.ds(0, slots - 1)],
        tile_recv_sem,
    ).wait()

    low_rows = window_len * low_pos
    near = [tile_in[start + k] for k in range(window_len + 2)]
    seen = [jnp.concatenate(near[k : k + window_len], 0) for k in range(3)]
    total = jnp.dot(seen[0], base_w[0], preferred_element_type=jnp.float32)
    total = total + jnp.dot(seen[1], base_w[1], preferred_element_type=jnp.float32)
    total = total + jnp.dot(seen[2], base_w[2], preferred_element_type=jnp.float32)
    half = total * 0.5
    base = (seen[1].astype(jnp.float32) + (half + half * jnp.tanh(half))).astype(jnp.bfloat16)
    projected = jnp.dot(base, cond_w[...], preferred_element_type=jnp.float32)
    for r in range(ratio):
        lifted[pl.ds(r, low_rows, stride=ratio), :] = projected

    loads["mlp_in"].wait()
    loads["mlp_out"].wait()
    for c in range(chunks):
        span = pl.ds(c * part, part)
        state = state_ref[:, span, :] + lifted[...].reshape(window_len, tile_pos, channels)[
            :, c * part : (c + 1) * part
        ]
        zeros_frame = jnp.zeros((1, part, channels), jnp.float32)
        for layer in range(layers):
            inverse = lax.rsqrt(jnp.mean(state * state, axis=-1, keepdims=True) + 1e-06)
            plain = state * inverse
            gain = gains[pl.ds(layer, 1), :] * 0.5
            taps = tconv[layer]
            before = (taps[0:1] * gain).reshape(1, 1, channels)
            here = (gain + taps[1:2] * gain).reshape(1, 1, channels)
            behind = (taps[2:3] * gain).reshape(1, 1, channels)
            mixed = (
                here * plain
                + before * jnp.concatenate([zeros_frame, plain[:-1]], 0)
                + behind * jnp.concatenate([plain[1:], zeros_frame], 0)
            )
            mixed = mixed.reshape(window_len * part, channels).astype(jnp.bfloat16)
            half = jnp.dot(mixed, mlp_in[layer], preferred_element_type=jnp.float32)
            hidden = (half + half * jnp.tanh(half)).astype(jnp.bfloat16)
            state = state + jnp.dot(
                hidden, mlp_out[layer], preferred_element_type=jnp.float32
            ).reshape(window_len, part, channels)
        refined[c] = state.astype(jnp.bfloat16)

        def place(frame, carry, c=c):
            frames_out[c, frame] = refined[c, jnp.clip(frame - start, 0, window_len - 1)]
            return carry

        each(slots, place)
        frames_in[c, me] = refined[c, jnp.clip(me - start, 0, window_len - 1)]

        def send_frame(step, carry, c=c):
            there = partner(step)
            pltpu.make_async_remote_copy(
                src_ref=frames_out.at[c, there],
                dst_ref=frames_in.at[c, me],
                send_sem=frame_send_sem.at[c],
                recv_sem=frame_recv_sem.at[c],
                device_id={AXIS: there},
                device_id_type=pl.DeviceIdType.MESH,
            ).start()
            return carry

        each(slots - 1, send_frame)

    scale = jnp.full((1, channels), 1.0, jnp.float32) / jnp.full((1, channels), denom, jnp.float32)
    for c in range(chunks):
        arrived = frames_in.at[c, pl.ds(0, slots - 1)]
        pltpu.make_async_copy(arrived, arrived, frame_recv_sem.at[c]).wait()

        def add(slot, sums, c=c):
            value = frames_in[c, slot].astype(jnp.float32)
            return tuple(
                sums[t] + weights[slot * tiles + t] * value for t in range(tiles)
            )

        sums = each(slots, add, tuple(jnp.zeros((part, channels), jnp.float32) for _ in range(tiles)))
        for t in range(tiles):
            out_ref[0, pl.ds(t * tile_pos + c * part, part), :] = (sums[t] * scale).astype(
                out_ref.dtype
            )

    sent = tile_out.at[pl.ds(0, slots - 1)]
    pltpu.make_async_copy(sent, sent, tile_send_sem).wait()
    for c in range(chunks):
        sent = frames_out.at[c, pl.ds(0, slots - 1)]
        pltpu.make_async_copy(sent, sent, frame_send_sem.at[c]).wait()


def slot_on_device(chunks, *args):
    (lowres, noisy, starts, blend, assign, base_w, cond_w, noise_w, gains, tconv, mlp_in,
     mlp_out) = args
    slots = assign.shape[0]
    windows = starts.shape[0]
    tiles = slots // windows
    _, window_len, tile_pos, channels = noisy.shape
    low_pos = lowres.shape[1] // tiles
    part = tile_pos // chunks
    half = jnp.bfloat16
    full = jnp.float32
    whole = jnp.int32
    return pl.pallas_call(
        functools.partial(slot_kernel, chunks),
        out_shape=jax.ShapeDtypeStruct((1, tiles * tile_pos, channels), half),
        in_specs=[pl.BlockSpec(memory_space=pltpu.HBM)] * len(args),
        out_specs=pl.BlockSpec(memory_space=pltpu.VMEM),
        scratch_shapes=[
            pltpu.VMEM((tiles, low_pos, channels), half),
            pltpu.VMEM(noisy.shape[1:], half),
            pltpu.SMEM(starts.shape, whole),
            pltpu.SMEM(blend.shape, whole),
            pltpu.SMEM(assign.shape, whole),
            pltpu.VMEM(base_w.shape, half),
            pltpu.VMEM(cond_w.shape, half),
            pltpu.VMEM(noise_w.shape, half),
            pltpu.VMEM(gains.shape, full),
            pltpu.VMEM(tconv.shape, full),
            pltpu.VMEM(mlp_in.shape, half),
            pltpu.VMEM(mlp_out.shape, half),
            pltpu.VMEM((slots, low_pos, channels), half),
            pltpu.VMEM((slots + 2, low_pos, channels), half),
            pltpu.VMEM((window_len, tile_pos, channels), full),
            pltpu.VMEM((window_len * tile_pos, channels), full),
            pltpu.VMEM((chunks, window_len, part, channels), half),
            pltpu.VMEM((chunks, slots, part, channels), half),
            pltpu.VMEM((chunks, slots, part, channels), half),
            pltpu.SMEM((slots * tiles,), full),
            pltpu.SemaphoreType.DMA((len(args),)),
            pltpu.SemaphoreType.DMA,
            pltpu.SemaphoreType.DMA,
            pltpu.SemaphoreType.DMA((chunks,)),
            pltpu.SemaphoreType.DMA((chunks,)),
        ],
        compiler_params=pltpu.CompilerParams(
            collective_id=0, has_side_effects=True, vmem_limit_bytes=60 * 1024 * 1024
        ),
    )(lowres.reshape(tiles, low_pos, channels), *args[1:])


def split_kernel(
    lowres_hbm, noisy_hbm, starts_hbm, blend_hbm, assign_hbm, base_w_hbm, cond_w_hbm, noise_w_hbm,
    gains_hbm, tconv_hbm, mlp_in_hbm, mlp_out_hbm,
    out_ref,
    lowres, noisy, starts, blend, assign, base_w, cond_w, noise_w, gains, tconv, mlp_in, mlp_out,
    low_out, low_in, noisy_wide, noisy_out, noisy_in, projected, shifted, cond_ref,
    video_out, matrices,
    load_sem, low_send, low_recv, noisy_send, noisy_recv, video_send, video_recv, own_sem,
):
    slots = assign.shape[0]
    windows, window_len = blend.shape
    tiles, low_pos, channels = lowres.shape
    tile_pos = noisy.shape[1]
    ratio = tile_pos // low_pos
    layers = gains.shape[0]
    me = lax.axis_index(AXIS)

    loads = {}
    for spot, (name, source, target) in enumerate((
        ("lowres", lowres_hbm, lowres),
        ("noisy", noisy_hbm.at[0], noisy),
        ("assign", assign_hbm, assign),
        ("starts", starts_hbm, starts),
        ("blend", blend_hbm, blend),
        ("base_w", base_w_hbm, base_w),
        ("cond_w", cond_w_hbm, cond_w),
        ("noise_w", noise_w_hbm, noise_w),
        ("gains", gains_hbm, gains),
        ("tconv", tconv_hbm, tconv),
        ("mlp_in", mlp_in_hbm, mlp_in),
        ("mlp_out", mlp_out_hbm, mlp_out),
    )):
        loads[name] = pltpu.make_async_copy(source, target, load_sem.at[spot])
    urgent = ("lowres", "noisy")
    for name in urgent:
        loads[name].start()

    half_slots = slots // 2
    side, place = me // half_slots, me % half_slots
    away = [
        (1 - side) * half_slots + lax.rem(place + step, half_slots) for step in range(half_slots)
    ]
    near = [
        side * half_slots + lax.rem(place + step, half_slots) for step in range(1, half_slots)
    ]
    partners = away + near

    barrier = pltpu.get_barrier_semaphore()
    for there in partners:
        pl.semaphore_signal(
            barrier, inc=1, device_id={AXIS: there}, device_id_type=pl.DeviceIdType.MESH
        )
    for name, load in loads.items():
        if name not in urgent:
            load.start()

    def send(source, target, there, send_sem, recv_sem):
        pltpu.make_async_remote_copy(
            src_ref=source, dst_ref=target, send_sem=send_sem, recv_sem=recv_sem,
            device_id={AXIS: there}, device_id_type=pl.DeviceIdType.MESH,
        ).start()

    def await_bytes(ref, sem):
        pltpu.make_async_copy(ref, ref, sem).wait()

    zero_slab = jnp.zeros((tiles, channels), jnp.float32)
    low_in[0] = zero_slab
    low_in[slots + 1] = zero_slab
    loads["lowres"].wait()
    for t in range(tiles):
        low_out[:, t, :] = lowres[t].astype(jnp.float32)
    low_in[me + 1] = low_out[me]

    pl.semaphore_wait(barrier, slots - 1)
    for there in partners:
        send(low_out.at[there], low_in.at[me + 1], there, low_send, low_recv)

    loads["noisy"].wait()
    noisy_wide[...] = noisy[...].reshape(window_len * tile_pos, channels).astype(jnp.float32)
    for j in range(slots):
        picked = [
            noisy_wide[pl.ds(j * ratio + r, window_len, stride=tile_pos), :] for r in range(ratio)
        ]
        noisy_out[j] = jnp.concatenate(picked, 0).astype(jnp.bfloat16)
    noisy_in[side, place] = noisy_out[me]

    for group, targets in enumerate((near, away)):
        for there in targets:
            send(
                noisy_out.at[there], noisy_in.at[side, place], there,
                noisy_send, noisy_recv.at[group],
            )

    for name in ("assign", "starts", "blend"):
        loads[name].wait()
    rows = slots * ratio * window_len
    lane = lax.broadcasted_iota(jnp.int32, (1, rows), 1)
    lane_slot = lane // (ratio * window_len)
    lane_pos = (lane // window_len) % ratio
    lane_step = lane % window_len
    first = jnp.zeros((1, rows), jnp.int32)
    lane_tile = jnp.zeros((1, rows), jnp.int32)
    lane_window = jnp.zeros((1, rows), jnp.int32)
    for d in range(slots):
        item = assign[d]
        here = lane_slot == d
        window = lax.div(item, tiles)
        lane_window = jnp.where(here, window, lane_window)
        lane_tile = jnp.where(here, lax.rem(item, tiles), lane_tile)
        first = jnp.where(here, starts[window], first)
    factor = jnp.zeros((1, rows), jnp.int32)
    for w in range(windows):
        for k in range(window_len):
            factor = jnp.where(
                jnp.logical_and(lane_window == w, lane_step == k), blend[w, k], factor
            )
    target = ((first + lane_step) * tiles + lane_tile) * ratio + lane_pos
    video_rows = slots * tiles * ratio
    row = lax.broadcasted_iota(jnp.int32, (video_rows, rows), 0)
    matrix = jnp.where(row == target, factor.astype(jnp.float32), 0.0)
    denom = jnp.sum(matrix, axis=1, keepdims=True)
    scale = 1.0 / denom
    half_rows = rows // 2
    for h in range(2):
        matrices[h] = matrix[:, h * half_rows : (h + 1) * half_rows].astype(jnp.bfloat16)

    for name in ("base_w", "cond_w", "noise_w", "gains", "tconv"):
        loads[name].wait()
    step_row = lax.broadcasted_iota(jnp.int32, (window_len, channels), 0)
    taps = []
    for layer in range(layers):
        gain = gains[pl.ds(layer, 1), :] * 0.5
        tap = tconv[layer]
        taps.append((
            jnp.where(step_row == 0, 0.0, tap[0:1] * gain),
            gain + tap[1:2] * gain,
            jnp.where(step_row == window_len - 1, 0.0, tap[2:3] * gain),
        ))
    await_bytes(low_in.at[pl.ds(0, slots - 1)], low_recv)
    total = None
    for k in range(3):
        seen = jnp.concatenate(
            [low_in[k : k + slots, t, :] for t in range(tiles)], 0
        )
        if k == 1:
            centre = seen
        term = jnp.dot(seen.astype(jnp.bfloat16), base_w[k], preferred_element_type=jnp.float32)
        total = term if total is None else total + term
    half = total * 0.5
    base = (centre + (half + half * jnp.tanh(half))).astype(jnp.bfloat16)
    projected[...] = jnp.dot(base, cond_w[...], preferred_element_type=jnp.float32)
    for t in range(tiles):
        for f in range(slots - window_len + 1):
            shifted[t, f] = projected[pl.ds(t * slots + f, window_len), :]
    for d in range(slots):
        item = assign[d]
        cond_ref[d // half_slots, d % half_slots, 0] = shifted[lax.rem(item, tiles), starts[lax.div(item, tiles)]]

    loads["mlp_in"].wait()
    loads["mlp_out"].wait()
    groups = half_slots * ratio
    video = None
    for group, chosen in enumerate((side, 1 - side)):
        await_bytes(noisy_in.at[0, pl.ds(0, half_slots - 1 + group)], noisy_recv.at[group])
        state = jnp.dot(
            noisy_in[chosen].reshape(half_rows, channels), noise_w[...],
            preferred_element_type=jnp.float32,
        ).reshape(half_slots, ratio, window_len, channels)
        state = (state + cond_ref[chosen]).reshape(groups, window_len, channels)
        for layer in range(layers):
            inverse = lax.rsqrt(jnp.mean(state * state, axis=-1, keepdims=True) + 1e-06)
            plain = state * inverse
            before, here, behind = taps[layer]
            mixed = (
                here[None] * plain
                + before[None] * pltpu.roll(plain, 1, 1)
                + behind[None] * pltpu.roll(plain, window_len - 1, 1)
            )
            mixed = mixed.reshape(half_rows, channels).astype(jnp.bfloat16)
            half = jnp.dot(mixed, mlp_in[layer], preferred_element_type=jnp.float32)
            hidden = (half + half * jnp.tanh(half)).astype(jnp.bfloat16)
            state = state + jnp.dot(
                hidden, mlp_out[layer], preferred_element_type=jnp.float32
            ).reshape(groups, window_len, channels)
        refined = state.reshape(half_rows, channels).astype(jnp.bfloat16)
        term = jnp.dot(matrices[chosen], refined, preferred_element_type=jnp.float32)
        video = term if video is None else video + term
    video = video * scale
    video_out[...] = video.astype(jnp.bfloat16).reshape(slots, tiles * ratio, channels)
    for there in partners:
        send(video_out.at[there], out_ref.at[me], there, video_send, video_recv)
    own = pltpu.make_async_copy(video_out.at[me], out_ref.at[me], own_sem)
    own.start()

    await_bytes(low_out.at[pl.ds(0, slots - 1)], low_send)
    await_bytes(noisy_out.at[pl.ds(0, slots - 1)], noisy_send)
    await_bytes(out_ref.at[pl.ds(0, slots - 1)], video_recv)
    own.wait()
    await_bytes(video_out.at[pl.ds(0, slots - 1)], video_send)


def order_kernel(tiles, video_ref, out_ref, wide, ordered):
    sources, rows, channels = video_ref.shape
    ratio = rows // tiles
    tile_pos = sources * ratio
    wide[...] = video_ref[...].reshape(sources * rows, channels).astype(jnp.float32)
    for t in range(tiles):
        for r in range(ratio):
            ordered[pl.ds(t * tile_pos + r, sources, stride=ratio), :] = wide[
                pl.ds(t * ratio + r, sources, stride=rows), :
            ]
    out_ref[0] = ordered[...].astype(out_ref.dtype)


def split_on_device(*args):
    (lowres, noisy, starts, blend, assign, base_w, cond_w, noise_w, gains, tconv, mlp_in,
     mlp_out) = args
    slots = assign.shape[0]
    tiles = slots // starts.shape[0]
    _, window_len, tile_pos, channels = noisy.shape
    low_pos = lowres.shape[1] // tiles
    ratio = tile_pos // low_pos
    rows = slots * ratio * window_len
    half, full, whole = jnp.bfloat16, jnp.float32, jnp.int32
    dma = pltpu.SemaphoreType.DMA
    video = pl.pallas_call(
        split_kernel,
        out_shape=jax.ShapeDtypeStruct((slots, tiles * ratio, channels), half),
        in_specs=[pl.BlockSpec(memory_space=pl.ANY)] * len(args),
        out_specs=pl.BlockSpec(memory_space=pl.ANY),
        scratch_shapes=[
            pltpu.VMEM((tiles, low_pos, channels), half),
            pltpu.VMEM(noisy.shape[1:], half),
            pltpu.SMEM(starts.shape, whole),
            pltpu.SMEM(blend.shape, whole),
            pltpu.SMEM(assign.shape, whole),
            pltpu.VMEM(base_w.shape, half),
            pltpu.VMEM(cond_w.shape, half),
            pltpu.VMEM(noise_w.shape, half),
            pltpu.VMEM(gains.shape, full),
            pltpu.VMEM(tconv.shape, full),
            pltpu.VMEM(mlp_in.shape, half),
            pltpu.VMEM(mlp_out.shape, half),
            pltpu.VMEM((slots, tiles, channels), full),
            pltpu.VMEM((slots + 2, tiles, channels), full),
            pltpu.VMEM((window_len * tile_pos, channels), full),
            pltpu.VMEM((slots, ratio * window_len, channels), half),
            pltpu.VMEM((2, slots // 2, ratio * window_len, channels), half),
            pltpu.VMEM((tiles * slots, channels), full),
            pltpu.VMEM((tiles, slots - window_len + 1, window_len, channels), full),
            pltpu.VMEM((2, slots // 2, 1, window_len, channels), full),
            pltpu.VMEM((slots, tiles * ratio, channels), half),
            pltpu.VMEM((2, slots * tiles * ratio, rows // 2), half),
            dma((len(args),)), dma, dma, dma, dma((2,)), dma, dma, dma,
        ],
        compiler_params=pltpu.CompilerParams(
            collective_id=0, has_side_effects=True, vmem_limit_bytes=60 * 1024 * 1024
        ),
    )(lowres.reshape(tiles, low_pos, channels), *args[1:])
    return pl.pallas_call(
        functools.partial(order_kernel, tiles),
        out_shape=jax.ShapeDtypeStruct((1, tiles * tile_pos, channels), half),
        in_specs=[pl.BlockSpec(memory_space=pltpu.VMEM)],
        out_specs=pl.BlockSpec(memory_space=pltpu.VMEM),
        scratch_shapes=[
            pltpu.VMEM((tiles * tile_pos, channels), full),
            pltpu.VMEM((tiles * tile_pos, channels), full),
        ],
        compiler_params=pltpu.CompilerParams(vmem_limit_bytes=60 * 1024 * 1024),
    )(video)


def on_device(*args):
    lowres, noisy, starts, _, assign = args[:5]
    slots = assign.shape[0]
    tiles = slots // starts.shape[0]
    low_pos = lowres.shape[1] // tiles
    ratio = noisy.shape[2] // low_pos
    if (
        low_pos == slots and slots % 2 == 0 and tiles <= SUBLANES and noisy.shape[1] == SUBLANES
        and (tiles * ratio) % 16 == 0
    ):
        return split_on_device(*args)
    return slot_on_device(2, *args)


def solution(mesh):
    in_specs = (
        P(("groups", AXIS), None, None),
        P(("groups", AXIS), None, None, None),
        P("groups"),
        P("groups", None),
        P("groups"),
        P(),
        P(),
        P(),
        P(),
        P(),
        P(),
        P(),
    )
    out_specs = P(("groups", AXIS), None, None)
    return jax.shard_map(
        on_device,
        mesh=mesh, in_specs=in_specs, out_specs=out_specs, check_vma=False
    )
```

```python
import functools

import jax
import jax.numpy as jnp
from jax import lax
from jax.experimental import pallas as pl
from jax.experimental.pallas import tpu as pltpu
from jax.sharding import PartitionSpec as P

AXIS = "frame"
UNROLL_UP_TO = 16
SUBLANES = 8


def each(count, body, carry=None):
    if count <= UNROLL_UP_TO:
        for index in range(count):
            carry = body(index, carry)
        return carry
    return lax.fori_loop(0, count, body, carry)


def slot_kernel(
    chunks,
    lowres_hbm, noisy_hbm, starts_hbm, blend_hbm, assign_hbm, base_w_hbm, cond_w_hbm, noise_w_hbm,
    gains_hbm, tconv_hbm, mlp_in_hbm, mlp_out_hbm,
    out_ref,
    lowres, noisy, starts, blend, assign, base_w, cond_w, noise_w, gains, tconv, mlp_in, mlp_out,
    tile_out, tile_in, state_ref, lifted, refined, frames_out, frames_in, weights,
    load_sem, tile_send_sem, tile_recv_sem, frame_send_sem, frame_recv_sem,
):
    slots = assign.shape[0]
    windows, window_len = blend.shape
    tiles = slots // windows
    tile_pos, channels = noisy.shape[1], noisy.shape[2]
    low_pos = lowres.shape[1]
    ratio = tile_pos // low_pos
    layers = gains.shape[0]
    part = tile_pos // chunks
    me = lax.axis_index(AXIS)

    loads = {}
    for spot, (name, source, target) in enumerate((
        ("assign", assign_hbm, assign),
        ("lowres", lowres_hbm, lowres),
        ("starts", starts_hbm, starts),
        ("blend", blend_hbm, blend),
        ("noisy", noisy_hbm.at[0], noisy),
        ("noise_w", noise_w_hbm, noise_w),
        ("base_w", base_w_hbm, base_w),
        ("cond_w", cond_w_hbm, cond_w),
        ("gains", gains_hbm, gains),
        ("tconv", tconv_hbm, tconv),
        ("mlp_in", mlp_in_hbm, mlp_in),
        ("mlp_out", mlp_out_hbm, mlp_out),
    )):
        loads[name] = pltpu.make_async_copy(source, target, load_sem.at[spot])
        loads[name].start()

    def partner(step):
        half = slots // 2
        offset = half + (step + 1) // 2 * (1 - 2 * (step % 2))
        return lax.rem(me + offset + slots, slots)

    barrier = pltpu.get_barrier_semaphore()

    def greet(step, carry):
        pl.semaphore_signal(
            barrier, inc=1, device_id={AXIS: partner(step)}, device_id_type=pl.DeviceIdType.MESH
        )
        return carry

    each(slots - 1, greet)

    zero_tile = jnp.zeros((low_pos, channels), tile_in.dtype)
    tile_in[0] = zero_tile
    tile_in[slots + 1] = zero_tile
    loads["assign"].wait()
    loads["lowres"].wait()

    def tile_for(slot):
        return lowres[lax.rem(assign[slot], tiles)]

    def pick(slot, carry):
        tile_out[slot] = tile_for(slot)
        return carry

    each(slots, pick)
    tile_in[me + 1] = tile_for(me)

    pl.semaphore_wait(barrier, slots - 1)

    def send_tile(step, carry):
        there = partner(step)
        pltpu.make_async_remote_copy(
            src_ref=tile_out.at[there],
            dst_ref=tile_in.at[me + 1],
            send_sem=tile_send_sem,
            recv_sem=tile_recv_sem,
            device_id={AXIS: there},
            device_id_type=pl.DeviceIdType.MESH,
        ).start()
        return carry

    each(slots - 1, send_tile)

    loads["noisy"].wait()
    loads["noise_w"].wait()
    rows = window_len * tile_pos
    state_ref[...] = jnp.dot(
        noisy[...].reshape(rows, channels), noise_w[...], preferred_element_type=jnp.float32
    ).reshape(window_len, tile_pos, channels)

    loads["starts"].wait()
    loads["blend"].wait()

    def weigh(slot, total):
        item = assign[slot]
        window = lax.div(item, tiles)
        tile = lax.rem(item, tiles)
        offset = me - starts[window]
        inside = jnp.logical_and(offset >= 0, offset < window_len)
        value = blend[window, jnp.clip(offset, 0, window_len - 1)]
        value = jnp.where(inside, value, 0)
        for t in range(tiles):
            weights[slot * tiles + t] = jnp.where(tile == t, value, 0).astype(jnp.float32)
        return total + jnp.where(tile == 0, value, 0)

    denom = each(slots, weigh, jnp.int32(0)).astype(jnp.float32)
    start = starts[lax.div(assign[me], tiles)]

    loads["gains"].wait()
    loads["tconv"].wait()
    loads["base_w"].wait()
    loads["cond_w"].wait()
    pltpu.make_async_copy(
        tile_in.at[pl.ds(0, slots - 1)],
        tile_in.at[pl.ds(0, slots - 1)],
        tile_recv_sem,
    ).wait()

    low_rows = window_len * low_pos
    near = [tile_in[start + k] for k in range(window_len + 2)]
    seen = [jnp.concatenate(near[k : k + window_len], 0) for k in range(3)]
    total = jnp.dot(seen[0], base_w[0], preferred_element_type=jnp.float32)
    total = total + jnp.dot(seen[1], base_w[1], preferred_element_type=jnp.float32)
    total = total + jnp.dot(seen[2], base_w[2], preferred_element_type=jnp.float32)
    half = total * 0.5
    base = (seen[1].astype(jnp.float32) + (half + half * jnp.tanh(half))).astype(jnp.bfloat16)
    projected = jnp.dot(base, cond_w[...], preferred_element_type=jnp.float32)
    for r in range(ratio):
        lifted[pl.ds(r, low_rows, stride=ratio), :] = projected

    loads["mlp_in"].wait()
    loads["mlp_out"].wait()
    for c in range(chunks):
        span = pl.ds(c * part, part)
        state = state_ref[:, span, :] + lifted[...].reshape(window_len, tile_pos, channels)[
            :, c * part : (c + 1) * part
        ]
        zeros_frame = jnp.zeros((1, part, channels), jnp.float32)
        for layer in range(layers):
            inverse = lax.rsqrt(jnp.mean(state * state, axis=-1, keepdims=True) + 1e-06)
            plain = state * inverse
            gain = gains[pl.ds(layer, 1), :] * 0.5
            taps = tconv[layer]
            before = (taps[0:1] * gain).reshape(1, 1, channels)
            here = (gain + taps[1:2] * gain).reshape(1, 1, channels)
            behind = (taps[2:3] * gain).reshape(1, 1, channels)
            mixed = (
                here * plain
                + before * jnp.concatenate([zeros_frame, plain[:-1]], 0)
                + behind * jnp.concatenate([plain[1:], zeros_frame], 0)
            )
            mixed = mixed.reshape(window_len * part, channels).astype(jnp.bfloat16)
            half = jnp.dot(mixed, mlp_in[layer], preferred_element_type=jnp.float32)
            hidden = (half + half * jnp.tanh(half)).astype(jnp.bfloat16)
            state = state + jnp.dot(
                hidden, mlp_out[layer], preferred_element_type=jnp.float32
            ).reshape(window_len, part, channels)
        refined[c] = state.astype(jnp.bfloat16)

        def place(frame, carry, c=c):
            frames_out[c, frame] = refined[c, jnp.clip(frame - start, 0, window_len - 1)]
            return carry

        each(slots, place)
        frames_in[c, me] = refined[c, jnp.clip(me - start, 0, window_len - 1)]

        def send_frame(step, carry, c=c):
            there = partner(step)
            pltpu.make_async_remote_copy(
                src_ref=frames_out.at[c, there],
                dst_ref=frames_in.at[c, me],
                send_sem=frame_send_sem.at[c],
                recv_sem=frame_recv_sem.at[c],
                device_id={AXIS: there},
                device_id_type=pl.DeviceIdType.MESH,
            ).start()
            return carry

        each(slots - 1, send_frame)

    scale = jnp.full((1, channels), 1.0, jnp.float32) / jnp.full((1, channels), denom, jnp.float32)
    for c in range(chunks):
        arrived = frames_in.at[c, pl.ds(0, slots - 1)]
        pltpu.make_async_copy(arrived, arrived, frame_recv_sem.at[c]).wait()

        def add(slot, sums, c=c):
            value = frames_in[c, slot].astype(jnp.float32)
            return tuple(
                sums[t] + weights[slot * tiles + t] * value for t in range(tiles)
            )

        sums = each(slots, add, tuple(jnp.zeros((part, channels), jnp.float32) for _ in range(tiles)))
        for t in range(tiles):
            out_ref[0, pl.ds(t * tile_pos + c * part, part), :] = (sums[t] * scale).astype(
                out_ref.dtype
            )

    sent = tile_out.at[pl.ds(0, slots - 1)]
    pltpu.make_async_copy(sent, sent, tile_send_sem).wait()
    for c in range(chunks):
        sent = frames_out.at[c, pl.ds(0, slots - 1)]
        pltpu.make_async_copy(sent, sent, frame_send_sem.at[c]).wait()


def slot_on_device(chunks, *args):
    (lowres, noisy, starts, blend, assign, base_w, cond_w, noise_w, gains, tconv, mlp_in,
     mlp_out) = args
    slots = assign.shape[0]
    windows = starts.shape[0]
    tiles = slots // windows
    _, window_len, tile_pos, channels = noisy.shape
    low_pos = lowres.shape[1] // tiles
    part = tile_pos // chunks
    half = jnp.bfloat16
    full = jnp.float32
    whole = jnp.int32
    return pl.pallas_call(
        functools.partial(slot_kernel, chunks),
        out_shape=jax.ShapeDtypeStruct((1, tiles * tile_pos, channels), half),
        in_specs=[pl.BlockSpec(memory_space=pltpu.HBM)] * len(args),
        out_specs=pl.BlockSpec(memory_space=pltpu.VMEM),
        scratch_shapes=[
            pltpu.VMEM((tiles, low_pos, channels), half),
            pltpu.VMEM(noisy.shape[1:], half),
            pltpu.SMEM(starts.shape, whole),
            pltpu.SMEM(blend.shape, whole),
            pltpu.SMEM(assign.shape, whole),
            pltpu.VMEM(base_w.shape, half),
            pltpu.VMEM(cond_w.shape, half),
            pltpu.VMEM(noise_w.shape, half),
            pltpu.VMEM(gains.shape, full),
            pltpu.VMEM(tconv.shape, full),
            pltpu.VMEM(mlp_in.shape, half),
            pltpu.VMEM(mlp_out.shape, half),
            pltpu.VMEM((slots, low_pos, channels), half),
            pltpu.VMEM((slots + 2, low_pos, channels), half),
            pltpu.VMEM((window_len, tile_pos, channels), full),
            pltpu.VMEM((window_len * tile_pos, channels), full),
            pltpu.VMEM((chunks, window_len, part, channels), half),
            pltpu.VMEM((chunks, slots, part, channels), half),
            pltpu.VMEM((chunks, slots, part, channels), half),
            pltpu.SMEM((slots * tiles,), full),
            pltpu.SemaphoreType.DMA((len(args),)),
            pltpu.SemaphoreType.DMA,
            pltpu.SemaphoreType.DMA,
            pltpu.SemaphoreType.DMA((chunks,)),
            pltpu.SemaphoreType.DMA((chunks,)),
        ],
        compiler_params=pltpu.CompilerParams(
            collective_id=0, has_side_effects=True, vmem_limit_bytes=60 * 1024 * 1024
        ),
    )(lowres.reshape(tiles, low_pos, channels), *args[1:])


def split_kernel(
    lowres_hbm, noisy_hbm, starts_hbm, blend_hbm, assign_hbm, base_w_hbm, cond_w_hbm, noise_w_hbm,
    gains_hbm, tconv_hbm, mlp_in_hbm, mlp_out_hbm,
    out_ref,
    lowres, noisy, starts, blend, assign, base_w, cond_w, noise_w, gains, tconv, mlp_in, mlp_out,
    low_out, low_in, noisy_wide, noisy_out, noisy_in, projected, shifted, cond_ref,
    video_out, matrices,
    load_sem, low_send, low_recv, noisy_send, noisy_recv, video_send, video_recv, own_sem,
):
    slots = assign.shape[0]
    windows, window_len = blend.shape
    tiles, low_pos, channels = lowres.shape
    tile_pos = noisy.shape[1]
    ratio = tile_pos // low_pos
    layers = gains.shape[0]
    me = lax.axis_index(AXIS)

    loads = {}
    for spot, (name, source, target) in enumerate((
        ("lowres", lowres_hbm, lowres),
        ("noisy", noisy_hbm.at[0], noisy),
        ("assign", assign_hbm, assign),
        ("starts", starts_hbm, starts),
        ("blend", blend_hbm, blend),
        ("base_w", base_w_hbm, base_w),
        ("cond_w", cond_w_hbm, cond_w),
        ("noise_w", noise_w_hbm, noise_w),
        ("gains", gains_hbm, gains),
        ("tconv", tconv_hbm, tconv),
        ("mlp_in", mlp_in_hbm, mlp_in),
        ("mlp_out", mlp_out_hbm, mlp_out),
    )):
        loads[name] = pltpu.make_async_copy(source, target, load_sem.at[spot])
    urgent = ("lowres", "noisy")
    for name in urgent:
        loads[name].start()

    half_slots = slots // 2
    side, place = me // half_slots, me % half_slots
    away = [
        (1 - side) * half_slots + lax.rem(place + step, half_slots) for step in range(half_slots)
    ]
    near = [
        side * half_slots + lax.rem(place + step, half_slots) for step in range(1, half_slots)
    ]
    partners = away + near

    barrier = pltpu.get_barrier_semaphore()
    for there in partners:
        pl.semaphore_signal(
            barrier, inc=1, device_id={AXIS: there}, device_id_type=pl.DeviceIdType.MESH
        )
    for name, load in loads.items():
        if name not in urgent:
            load.start()

    def send(source, target, there, send_sem, recv_sem):
        pltpu.make_async_remote_copy(
            src_ref=source, dst_ref=target, send_sem=send_sem, recv_sem=recv_sem,
            device_id={AXIS: there}, device_id_type=pl.DeviceIdType.MESH,
        ).start()

    def await_bytes(ref, sem):
        pltpu.make_async_copy(ref, ref, sem).wait()

    zero_slab = jnp.zeros((tiles, channels), jnp.float32)
    low_in[0] = zero_slab
    low_in[slots + 1] = zero_slab
    loads["lowres"].wait()
    for t in range(tiles):
        low_out[:, t, :] = lowres[t].astype(jnp.float32)
    low_in[me + 1] = low_out[me]

    loads["noisy"].wait()
    noisy_wide[...] = noisy[...].reshape(window_len * tile_pos, channels).astype(jnp.float32)
    for j in range(slots):
        picked = [
            noisy_wide[pl.ds(j * ratio + r, window_len, stride=tile_pos), :] for r in range(ratio)
        ]
        noisy_out[j] = jnp.concatenate(picked, 0).astype(jnp.bfloat16)
    noisy_in[side, place] = noisy_out[me]

    pl.semaphore_wait(barrier, slots - 1)
    for there in partners:
        send(low_out.at[there], low_in.at[me + 1], there, low_send, low_recv)

    for group, targets in enumerate((near, away)):
        for there in targets:
            send(
                noisy_out.at[there], noisy_in.at[side, place], there,
                noisy_send, noisy_recv.at[group],
            )

    for name in ("assign", "starts", "blend"):
        loads[name].wait()
    rows = slots * ratio * window_len
    lane = lax.broadcasted_iota(jnp.int32, (1, rows), 1)
    lane_slot = lane // (ratio * window_len)
    lane_pos = (lane // window_len) % ratio
    lane_step = lane % window_len
    first = jnp.zeros((1, rows), jnp.int32)
    lane_tile = jnp.zeros((1, rows), jnp.int32)
    lane_window = jnp.zeros((1, rows), jnp.int32)
    for d in range(slots):
        item = assign[d]
        here = lane_slot == d
        window = lax.div(item, tiles)
        lane_window = jnp.where(here, window, lane_window)
        lane_tile = jnp.where(here, lax.rem(item, tiles), lane_tile)
        first = jnp.where(here, starts[window], first)
    factor = jnp.zeros((1, rows), jnp.int32)
    for w in range(windows):
        for k in range(window_len):
            factor = jnp.where(
                jnp.logical_and(lane_window == w, lane_step == k), blend[w, k], factor
            )
    target = ((first + lane_step) * tiles + lane_tile) * ratio + lane_pos
    video_rows = slots * tiles * ratio
    row = lax.broadcasted_iota(jnp.int32, (video_rows, rows), 0)
    matrix = jnp.where(row == target, factor.astype(jnp.float32), 0.0)
    denom = jnp.sum(matrix, axis=1, keepdims=True)
    scale = 1.0 / denom
    half_rows = rows // 2
    for h in range(2):
        matrices[h] = matrix[:, h * half_rows : (h + 1) * half_rows].astype(jnp.bfloat16)

    for name in ("base_w", "cond_w", "noise_w", "gains", "tconv"):
        loads[name].wait()
    step_row = lax.broadcasted_iota(jnp.int32, (window_len, channels), 0)
    taps = []
    for layer in range(layers):
        gain = gains[pl.ds(layer, 1), :] * 0.5
        tap = tconv[layer]
        taps.append((
            jnp.where(step_row == 0, 0.0, tap[0:1] * gain),
            gain + tap[1:2] * gain,
            jnp.where(step_row == window_len - 1, 0.0, tap[2:3] * gain),
        ))
    await_bytes(low_in.at[pl.ds(0, slots - 1)], low_recv)
    total = None
    for k in range(3):
        seen = jnp.concatenate(
            [low_in[k : k + slots, t, :] for t in range(tiles)], 0
        )
        if k == 1:
            centre = seen
        term = jnp.dot(seen.astype(jnp.bfloat16), base_w[k], preferred_element_type=jnp.float32)
        total = term if total is None else total + term
    half = total * 0.5
    base = (centre + (half + half * jnp.tanh(half))).astype(jnp.bfloat16)
    projected[...] = jnp.dot(base, cond_w[...], preferred_element_type=jnp.float32)
    for t in range(tiles):
        for f in range(slots - window_len + 1):
            shifted[t, f] = projected[pl.ds(t * slots + f, window_len), :]
    for d in range(slots):
        item = assign[d]
        cond_ref[d // half_slots, d % half_slots, 0] = shifted[lax.rem(item, tiles), starts[lax.div(item, tiles)]]

    loads["mlp_in"].wait()
    loads["mlp_out"].wait()
    groups = half_slots * ratio
    video = None
    for group, chosen in enumerate((side, 1 - side)):
        await_bytes(noisy_in.at[0, pl.ds(0, half_slots - 1 + group)], noisy_recv.at[group])
        state = jnp.dot(
            noisy_in[chosen].reshape(half_rows, channels), noise_w[...],
            preferred_element_type=jnp.float32,
        ).reshape(half_slots, ratio, window_len, channels)
        state = (state + cond_ref[chosen]).reshape(groups, window_len, channels)
        for layer in range(layers):
            inverse = lax.rsqrt(jnp.mean(state * state, axis=-1, keepdims=True) + 1e-06)
            plain = state * inverse
            before, here, behind = taps[layer]
            mixed = (
                here[None] * plain
                + before[None] * pltpu.roll(plain, 1, 1)
                + behind[None] * pltpu.roll(plain, window_len - 1, 1)
            )
            mixed = mixed.reshape(half_rows, channels).astype(jnp.bfloat16)
            half = jnp.dot(mixed, mlp_in[layer], preferred_element_type=jnp.float32)
            hidden = (half + half * jnp.tanh(half)).astype(jnp.bfloat16)
            state = state + jnp.dot(
                hidden, mlp_out[layer], preferred_element_type=jnp.float32
            ).reshape(groups, window_len, channels)
        refined = state.reshape(half_rows, channels).astype(jnp.bfloat16)
        term = jnp.dot(matrices[chosen], refined, preferred_element_type=jnp.float32)
        video = term if video is None else video + term
    video = video * scale
    video_out[...] = video.astype(jnp.bfloat16).reshape(slots, tiles * ratio, channels)
    for there in partners:
        send(video_out.at[there], out_ref.at[me], there, video_send, video_recv)
    own = pltpu.make_async_copy(video_out.at[me], out_ref.at[me], own_sem)
    own.start()

    await_bytes(low_out.at[pl.ds(0, slots - 1)], low_send)
    await_bytes(noisy_out.at[pl.ds(0, slots - 1)], noisy_send)
    await_bytes(out_ref.at[pl.ds(0, slots - 1)], video_recv)
    own.wait()
    await_bytes(video_out.at[pl.ds(0, slots - 1)], video_send)


def order_kernel(tiles, video_ref, out_ref, wide, ordered):
    sources, rows, channels = video_ref.shape
    ratio = rows // tiles
    tile_pos = sources * ratio
    wide[...] = video_ref[...].reshape(sources * rows, channels).astype(jnp.float32)
    for t in range(tiles):
        for r in range(ratio):
            ordered[pl.ds(t * tile_pos + r, sources, stride=ratio), :] = wide[
                pl.ds(t * ratio + r, sources, stride=rows), :
            ]
    out_ref[0] = ordered[...].astype(out_ref.dtype)


def split_on_device(*args):
    (lowres, noisy, starts, blend, assign, base_w, cond_w, noise_w, gains, tconv, mlp_in,
     mlp_out) = args
    slots = assign.shape[0]
    tiles = slots // starts.shape[0]
    _, window_len, tile_pos, channels = noisy.shape
    low_pos = lowres.shape[1] // tiles
    ratio = tile_pos // low_pos
    rows = slots * ratio * window_len
    half, full, whole = jnp.bfloat16, jnp.float32, jnp.int32
    dma = pltpu.SemaphoreType.DMA
    video = pl.pallas_call(
        split_kernel,
        out_shape=jax.ShapeDtypeStruct((slots, tiles * ratio, channels), half),
        in_specs=[pl.BlockSpec(memory_space=pl.ANY)] * len(args),
        out_specs=pl.BlockSpec(memory_space=pl.ANY),
        scratch_shapes=[
            pltpu.VMEM((tiles, low_pos, channels), half),
            pltpu.VMEM(noisy.shape[1:], half),
            pltpu.SMEM(starts.shape, whole),
            pltpu.SMEM(blend.shape, whole),
            pltpu.SMEM(assign.shape, whole),
            pltpu.VMEM(base_w.shape, half),
            pltpu.VMEM(cond_w.shape, half),
            pltpu.VMEM(noise_w.shape, half),
            pltpu.VMEM(gains.shape, full),
            pltpu.VMEM(tconv.shape, full),
            pltpu.VMEM(mlp_in.shape, half),
            pltpu.VMEM(mlp_out.shape, half),
            pltpu.VMEM((slots, tiles, channels), full),
            pltpu.VMEM((slots + 2, tiles, channels), full),
            pltpu.VMEM((window_len * tile_pos, channels), full),
            pltpu.VMEM((slots, ratio * window_len, channels), half),
            pltpu.VMEM((2, slots // 2, ratio * window_len, channels), half),
            pltpu.VMEM((tiles * slots, channels), full),
            pltpu.VMEM((tiles, slots - window_len + 1, window_len, channels), full),
            pltpu.VMEM((2, slots // 2, 1, window_len, channels), full),
            pltpu.VMEM((slots, tiles * ratio, channels), half),
            pltpu.VMEM((2, slots * tiles * ratio, rows // 2), half),
            dma((len(args),)), dma, dma, dma, dma((2,)), dma, dma, dma,
        ],
        compiler_params=pltpu.CompilerParams(
            collective_id=0, has_side_effects=True, vmem_limit_bytes=60 * 1024 * 1024
        ),
    )(lowres.reshape(tiles, low_pos, channels), *args[1:])
    return pl.pallas_call(
        functools.partial(order_kernel, tiles),
        out_shape=jax.ShapeDtypeStruct((1, tiles * tile_pos, channels), half),
        in_specs=[pl.BlockSpec(memory_space=pltpu.VMEM)],
        out_specs=pl.BlockSpec(memory_space=pltpu.VMEM),
        scratch_shapes=[
            pltpu.VMEM((tiles * tile_pos, channels), full),
            pltpu.VMEM((tiles * tile_pos, channels), full),
        ],
        compiler_params=pltpu.CompilerParams(vmem_limit_bytes=60 * 1024 * 1024),
    )(video)


def on_device(*args):
    lowres, noisy, starts, _, assign = args[:5]
    slots = assign.shape[0]
    tiles = slots // starts.shape[0]
    low_pos = lowres.shape[1] // tiles
    ratio = noisy.shape[2] // low_pos
    if (
        low_pos == slots and slots % 2 == 0 and tiles <= SUBLANES and noisy.shape[1] == SUBLANES
        and (tiles * ratio) % 16 == 0
    ):
        return split_on_device(*args)
    return slot_on_device(2, *args)


def solution(mesh):
    in_specs = (
        P(("groups", AXIS), None, None),
        P(("groups", AXIS), None, None, None),
        P("groups"),
        P("groups", None),
        P("groups"),
        P(),
        P(),
        P(),
        P(),
        P(),
        P(),
        P(),
    )
    out_specs = P(("groups", AXIS), None, None)
    return jax.shard_map(
        on_device,
        mesh=mesh, in_specs=in_specs, out_specs=out_specs, check_vma=False
    )
```

```python
import functools

import jax
import jax.numpy as jnp
from jax import lax
from jax.experimental import pallas as pl
from jax.experimental.pallas import tpu as pltpu
from jax.sharding import PartitionSpec as P

AXIS = "frame"
UNROLL_UP_TO = 16
SUBLANES = 8


def each(count, body, carry=None):
    if count <= UNROLL_UP_TO:
        for index in range(count):
            carry = body(index, carry)
        return carry
    return lax.fori_loop(0, count, body, carry)


def slot_kernel(
    chunks,
    lowres_hbm, noisy_hbm, starts_hbm, blend_hbm, assign_hbm, base_w_hbm, cond_w_hbm, noise_w_hbm,
    gains_hbm, tconv_hbm, mlp_in_hbm, mlp_out_hbm,
    out_ref,
    lowres, noisy, starts, blend, assign, base_w, cond_w, noise_w, gains, tconv, mlp_in, mlp_out,
    tile_out, tile_in, state_ref, lifted, refined, frames_out, frames_in, weights,
    load_sem, tile_send_sem, tile_recv_sem, frame_send_sem, frame_recv_sem,
):
    slots = assign.shape[0]
    windows, window_len = blend.shape
    tiles = slots // windows
    tile_pos, channels = noisy.shape[1], noisy.shape[2]
    low_pos = lowres.shape[1]
    ratio = tile_pos // low_pos
    layers = gains.shape[0]
    part = tile_pos // chunks
    me = lax.axis_index(AXIS)

    loads = {}
    for spot, (name, source, target) in enumerate((
        ("assign", assign_hbm, assign),
        ("lowres", lowres_hbm, lowres),
        ("starts", starts_hbm, starts),
        ("blend", blend_hbm, blend),
        ("noisy", noisy_hbm.at[0], noisy),
        ("noise_w", noise_w_hbm, noise_w),
        ("base_w", base_w_hbm, base_w),
        ("cond_w", cond_w_hbm, cond_w),
        ("gains", gains_hbm, gains),
        ("tconv", tconv_hbm, tconv),
        ("mlp_in", mlp_in_hbm, mlp_in),
        ("mlp_out", mlp_out_hbm, mlp_out),
    )):
        loads[name] = pltpu.make_async_copy(source, target, load_sem.at[spot])
        loads[name].start()

    def partner(step):
        half = slots // 2
        offset = half + (step + 1) // 2 * (1 - 2 * (step % 2))
        return lax.rem(me + offset + slots, slots)

    barrier = pltpu.get_barrier_semaphore()

    def greet(step, carry):
        pl.semaphore_signal(
            barrier, inc=1, device_id={AXIS: partner(step)}, device_id_type=pl.DeviceIdType.MESH
        )
        return carry

    each(slots - 1, greet)

    zero_tile = jnp.zeros((low_pos, channels), tile_in.dtype)
    tile_in[0] = zero_tile
    tile_in[slots + 1] = zero_tile
    loads["assign"].wait()
    loads["lowres"].wait()

    def tile_for(slot):
        return lowres[lax.rem(assign[slot], tiles)]

    def pick(slot, carry):
        tile_out[slot] = tile_for(slot)
        return carry

    each(slots, pick)
    tile_in[me + 1] = tile_for(me)

    pl.semaphore_wait(barrier, slots - 1)

    def send_tile(step, carry):
        there = partner(step)
        pltpu.make_async_remote_copy(
            src_ref=tile_out.at[there],
            dst_ref=tile_in.at[me + 1],
            send_sem=tile_send_sem,
            recv_sem=tile_recv_sem,
            device_id={AXIS: there},
            device_id_type=pl.DeviceIdType.MESH,
        ).start()
        return carry

    each(slots - 1, send_tile)

    loads["noisy"].wait()
    loads["noise_w"].wait()
    rows = window_len * tile_pos
    state_ref[...] = jnp.dot(
        noisy[...].reshape(rows, channels), noise_w[...], preferred_element_type=jnp.float32
    ).reshape(window_len, tile_pos, channels)

    loads["starts"].wait()
    loads["blend"].wait()

    def weigh(slot, total):
        item = assign[slot]
        window = lax.div(item, tiles)
        tile = lax.rem(item, tiles)
        offset = me - starts[window]
        inside = jnp.logical_and(offset >= 0, offset < window_len)
        value = blend[window, jnp.clip(offset, 0, window_len - 1)]
        value = jnp.where(inside, value, 0)
        for t in range(tiles):
            weights[slot * tiles + t] = jnp.where(tile == t, value, 0).astype(jnp.float32)
        return total + jnp.where(tile == 0, value, 0)

    denom = each(slots, weigh, jnp.int32(0)).astype(jnp.float32)
    start = starts[lax.div(assign[me], tiles)]

    loads["gains"].wait()
    loads["tconv"].wait()
    loads["base_w"].wait()
    loads["cond_w"].wait()
    pltpu.make_async_copy(
        tile_in.at[pl.ds(0, slots - 1)],
        tile_in.at[pl.ds(0, slots - 1)],
        tile_recv_sem,
    ).wait()

    low_rows = window_len * low_pos
    near = [tile_in[start + k] for k in range(window_len + 2)]
    seen = [jnp.concatenate(near[k : k + window_len], 0) for k in range(3)]
    total = jnp.dot(seen[0], base_w[0], preferred_element_type=jnp.float32)
    total = total + jnp.dot(seen[1], base_w[1], preferred_element_type=jnp.float32)
    total = total + jnp.dot(seen[2], base_w[2], preferred_element_type=jnp.float32)
    half = total * 0.5
    base = (seen[1].astype(jnp.float32) + (half + half * jnp.tanh(half))).astype(jnp.bfloat16)
    projected = jnp.dot(base, cond_w[...], preferred_element_type=jnp.float32)
    for r in range(ratio):
        lifted[pl.ds(r, low_rows, stride=ratio), :] = projected

    loads["mlp_in"].wait()
    loads["mlp_out"].wait()
    for c in range(chunks):
        span = pl.ds(c * part, part)
        state = state_ref[:, span, :] + lifted[...].reshape(window_len, tile_pos, channels)[
            :, c * part : (c + 1) * part
        ]
        zeros_frame = jnp.zeros((1, part, channels), jnp.float32)
        for layer in range(layers):
            inverse = lax.rsqrt(jnp.mean(state * state, axis=-1, keepdims=True) + 1e-06)
            plain = state * inverse
            gain = gains[pl.ds(layer, 1), :] * 0.5
            taps = tconv[layer]
            before = (taps[0:1] * gain).reshape(1, 1, channels)
            here = (gain + taps[1:2] * gain).reshape(1, 1, channels)
            behind = (taps[2:3] * gain).reshape(1, 1, channels)
            mixed = (
                here * plain
                + before * jnp.concatenate([zeros_frame, plain[:-1]], 0)
                + behind * jnp.concatenate([plain[1:], zeros_frame], 0)
            )
            mixed = mixed.reshape(window_len * part, channels).astype(jnp.bfloat16)
            half = jnp.dot(mixed, mlp_in[layer], preferred_element_type=jnp.float32)
            hidden = (half + half * jnp.tanh(half)).astype(jnp.bfloat16)
            state = state + jnp.dot(
                hidden, mlp_out[layer], preferred_element_type=jnp.float32
            ).reshape(window_len, part, channels)
        refined[c] = state.astype(jnp.bfloat16)

        def place(frame, carry, c=c):
            frames_out[c, frame] = refined[c, jnp.clip(frame - start, 0, window_len - 1)]
            return carry

        each(slots, place)
        frames_in[c, me] = refined[c, jnp.clip(me - start, 0, window_len - 1)]

        def send_frame(step, carry, c=c):
            there = partner(step)
            pltpu.make_async_remote_copy(
                src_ref=frames_out.at[c, there],
                dst_ref=frames_in.at[c, me],
                send_sem=frame_send_sem.at[c],
                recv_sem=frame_recv_sem.at[c],
                device_id={AXIS: there},
                device_id_type=pl.DeviceIdType.MESH,
            ).start()
            return carry

        each(slots - 1, send_frame)

    scale = jnp.full((1, channels), 1.0, jnp.float32) / jnp.full((1, channels), denom, jnp.float32)
    for c in range(chunks):
        arrived = frames_in.at[c, pl.ds(0, slots - 1)]
        pltpu.make_async_copy(arrived, arrived, frame_recv_sem.at[c]).wait()

        def add(slot, sums, c=c):
            value = frames_in[c, slot].astype(jnp.float32)
            return tuple(
                sums[t] + weights[slot * tiles + t] * value for t in range(tiles)
            )

        sums = each(slots, add, tuple(jnp.zeros((part, channels), jnp.float32) for _ in range(tiles)))
        for t in range(tiles):
            out_ref[0, pl.ds(t * tile_pos + c * part, part), :] = (sums[t] * scale).astype(
                out_ref.dtype
            )

    sent = tile_out.at[pl.ds(0, slots - 1)]
    pltpu.make_async_copy(sent, sent, tile_send_sem).wait()
    for c in range(chunks):
        sent = frames_out.at[c, pl.ds(0, slots - 1)]
        pltpu.make_async_copy(sent, sent, frame_send_sem.at[c]).wait()


def slot_on_device(chunks, *args):
    (lowres, noisy, starts, blend, assign, base_w, cond_w, noise_w, gains, tconv, mlp_in,
     mlp_out) = args
    slots = assign.shape[0]
    windows = starts.shape[0]
    tiles = slots // windows
    _, window_len, tile_pos, channels = noisy.shape
    low_pos = lowres.shape[1] // tiles
    part = tile_pos // chunks
    half = jnp.bfloat16
    full = jnp.float32
    whole = jnp.int32
    return pl.pallas_call(
        functools.partial(slot_kernel, chunks),
        out_shape=jax.ShapeDtypeStruct((1, tiles * tile_pos, channels), half),
        in_specs=[pl.BlockSpec(memory_space=pltpu.HBM)] * len(args),
        out_specs=pl.BlockSpec(memory_space=pltpu.VMEM),
        scratch_shapes=[
            pltpu.VMEM((tiles, low_pos, channels), half),
            pltpu.VMEM(noisy.shape[1:], half),
            pltpu.SMEM(starts.shape, whole),
            pltpu.SMEM(blend.shape, whole),
            pltpu.SMEM(assign.shape, whole),
            pltpu.VMEM(base_w.shape, half),
            pltpu.VMEM(cond_w.shape, half),
            pltpu.VMEM(noise_w.shape, half),
            pltpu.VMEM(gains.shape, full),
            pltpu.VMEM(tconv.shape, full),
            pltpu.VMEM(mlp_in.shape, half),
            pltpu.VMEM(mlp_out.shape, half),
            pltpu.VMEM((slots, low_pos, channels), half),
            pltpu.VMEM((slots + 2, low_pos, channels), half),
            pltpu.VMEM((window_len, tile_pos, channels), full),
            pltpu.VMEM((window_len * tile_pos, channels), full),
            pltpu.VMEM((chunks, window_len, part, channels), half),
            pltpu.VMEM((chunks, slots, part, channels), half),
            pltpu.VMEM((chunks, slots, part, channels), half),
            pltpu.SMEM((slots * tiles,), full),
            pltpu.SemaphoreType.DMA((len(args),)),
            pltpu.SemaphoreType.DMA,
            pltpu.SemaphoreType.DMA,
            pltpu.SemaphoreType.DMA((chunks,)),
            pltpu.SemaphoreType.DMA((chunks,)),
        ],
        compiler_params=pltpu.CompilerParams(
            collective_id=0, has_side_effects=True, vmem_limit_bytes=60 * 1024 * 1024
        ),
    )(lowres.reshape(tiles, low_pos, channels), *args[1:])


def split_kernel(
    lowres_hbm, noisy_hbm, starts_hbm, blend_hbm, assign_hbm, base_w_hbm, cond_w_hbm, noise_w_hbm,
    gains_hbm, tconv_hbm, mlp_in_hbm, mlp_out_hbm,
    out_ref,
    lowres, noisy, starts, blend, assign, base_w, cond_w, noise_w, gains, tconv, mlp_in, mlp_out,
    low_out, low_in, noisy_wide, noisy_out, noisy_in, projected, shifted, cond_ref,
    video_out, matrices,
    load_sem, low_send, low_recv, noisy_send, noisy_recv, video_send, video_recv, own_sem,
):
    slots = assign.shape[0]
    windows, window_len = blend.shape
    tiles, low_pos, channels = lowres.shape
    tile_pos = noisy.shape[1]
    ratio = tile_pos // low_pos
    layers = gains.shape[0]
    me = lax.axis_index(AXIS)

    loads = {}
    for spot, (name, source, target) in enumerate((
        ("lowres", lowres_hbm, lowres),
        ("noisy", noisy_hbm.at[0], noisy),
        ("assign", assign_hbm, assign),
        ("starts", starts_hbm, starts),
        ("blend", blend_hbm, blend),
        ("base_w", base_w_hbm, base_w),
        ("cond_w", cond_w_hbm, cond_w),
        ("noise_w", noise_w_hbm, noise_w),
        ("gains", gains_hbm, gains),
        ("tconv", tconv_hbm, tconv),
        ("mlp_in", mlp_in_hbm, mlp_in),
        ("mlp_out", mlp_out_hbm, mlp_out),
    )):
        loads[name] = pltpu.make_async_copy(source, target, load_sem.at[spot])
    urgent = ("lowres", "noisy")
    for name in urgent:
        loads[name].start()

    half_slots = slots // 2
    side, place = me // half_slots, me % half_slots
    away = [
        (1 - side) * half_slots + lax.rem(place + step, half_slots) for step in range(half_slots)
    ]
    near = [
        side * half_slots + lax.rem(place + step, half_slots) for step in range(1, half_slots)
    ]
    partners = away + near

    barrier = pltpu.get_barrier_semaphore()
    for there in partners:
        pl.semaphore_signal(
            barrier, inc=1, device_id={AXIS: there}, device_id_type=pl.DeviceIdType.MESH
        )
    for name, load in loads.items():
        if name not in urgent:
            load.start()

    def send(source, target, there, send_sem, recv_sem):
        pltpu.make_async_remote_copy(
            src_ref=source, dst_ref=target, send_sem=send_sem, recv_sem=recv_sem,
            device_id={AXIS: there}, device_id_type=pl.DeviceIdType.MESH,
        ).start()

    def await_bytes(ref, sem):
        pltpu.make_async_copy(ref, ref, sem).wait()

    zero_slab = jnp.zeros((tiles, channels), jnp.float32)
    low_in[0] = zero_slab
    low_in[slots + 1] = zero_slab
    loads["lowres"].wait()
    for t in range(tiles):
        low_out[:, t, :] = lowres[t].astype(jnp.float32)
    low_in[me + 1] = low_out[me]

    loads["noisy"].wait()
    noisy_wide[...] = noisy[...].reshape(window_len * tile_pos, channels).astype(jnp.float32)
    for j in range(slots):
        picked = [
            noisy_wide[pl.ds(j * ratio + r, window_len, stride=tile_pos), :] for r in range(ratio)
        ]
        noisy_out[j] = jnp.concatenate(picked, 0).astype(jnp.bfloat16)
    noisy_in[side, place] = noisy_out[me]

    pl.semaphore_wait(barrier, slots - 1)
    for there in partners:
        send(low_out.at[there], low_in.at[me + 1], there, low_send, low_recv)

    for group, targets in enumerate((near, away)):
        for there in targets:
            send(
                noisy_out.at[there], noisy_in.at[side, place], there,
                noisy_send, noisy_recv.at[group],
            )

    for name in ("assign", "starts", "blend"):
        loads[name].wait()
    rows = slots * ratio * window_len
    lane = lax.broadcasted_iota(jnp.int32, (1, rows), 1)
    lane_slot = lane // (ratio * window_len)
    lane_pos = (lane // window_len) % ratio
    lane_step = lane % window_len
    first = jnp.zeros((1, rows), jnp.int32)
    lane_tile = jnp.zeros((1, rows), jnp.int32)
    lane_window = jnp.zeros((1, rows), jnp.int32)
    for d in range(slots):
        item = assign[d]
        here = lane_slot == d
        window = lax.div(item, tiles)
        lane_window = jnp.where(here, window, lane_window)
        lane_tile = jnp.where(here, lax.rem(item, tiles), lane_tile)
        first = jnp.where(here, starts[window], first)
    factor = jnp.zeros((1, rows), jnp.int32)
    for w in range(windows):
        for k in range(window_len):
            factor = jnp.where(
                jnp.logical_and(lane_window == w, lane_step == k), blend[w, k], factor
            )
    target = ((first + lane_step) * tiles + lane_tile) * ratio + lane_pos
    video_rows = slots * tiles * ratio
    row = lax.broadcasted_iota(jnp.int32, (video_rows, rows), 0)
    matrix = jnp.where(row == target, factor.astype(jnp.float32), 0.0)
    denom = jnp.sum(matrix, axis=1, keepdims=True)
    scale = 1.0 / denom
    half_rows = rows // 2
    for h in range(2):
        matrices[h] = matrix[:, h * half_rows : (h + 1) * half_rows].astype(jnp.bfloat16)

    for name in ("base_w", "cond_w", "noise_w", "gains", "tconv"):
        loads[name].wait()
    step_row = lax.broadcasted_iota(jnp.int32, (window_len, channels), 0)
    taps = []
    for layer in range(layers):
        gain = gains[pl.ds(layer, 1), :] * 0.5
        tap = tconv[layer]
        taps.append((
            jnp.where(step_row == 0, 0.0, tap[0:1] * gain),
            gain + tap[1:2] * gain,
            jnp.where(step_row == window_len - 1, 0.0, tap[2:3] * gain),
        ))
    await_bytes(low_in.at[pl.ds(0, slots - 1)], low_recv)
    total = None
    for k in range(3):
        seen = jnp.concatenate(
            [low_in[k : k + slots, t, :] for t in range(tiles)], 0
        )
        if k == 1:
            centre = seen
        term = jnp.dot(seen.astype(jnp.bfloat16), base_w[k], preferred_element_type=jnp.float32)
        total = term if total is None else total + term
    half = total * 0.5
    base = (centre + (half + half * jnp.tanh(half))).astype(jnp.bfloat16)
    projected[...] = jnp.dot(base, cond_w[...], preferred_element_type=jnp.float32)
    for t in range(tiles):
        for f in range(slots - window_len + 1):
            shifted[t, f] = projected[pl.ds(t * slots + f, window_len), :]
    for d in range(slots):
        item = assign[d]
        cond_ref[d // half_slots, d % half_slots, 0] = shifted[lax.rem(item, tiles), starts[lax.div(item, tiles)]]

    loads["mlp_in"].wait()
    loads["mlp_out"].wait()
    groups = half_slots * ratio
    video = None
    for group, chosen in enumerate((side, 1 - side)):
        await_bytes(noisy_in.at[0, pl.ds(0, half_slots - 1 + group)], noisy_recv.at[group])
        state = jnp.dot(
            noisy_in[chosen].reshape(half_rows, channels), noise_w[...],
            preferred_element_type=jnp.float32,
        ).reshape(half_slots, ratio, window_len, channels)
        state = (state + cond_ref[chosen]).reshape(groups, window_len, channels)
        for layer in range(layers):
            inverse = lax.rsqrt(jnp.mean(state * state, axis=-1, keepdims=True) + 1e-06)
            plain = state * inverse
            before, here, behind = taps[layer]
            mixed = (
                here[None] * plain
                + before[None] * pltpu.roll(plain, 1, 1)
                + behind[None] * pltpu.roll(plain, window_len - 1, 1)
            )
            mixed = mixed.reshape(half_rows, channels).astype(jnp.bfloat16)
            half = jnp.dot(mixed, mlp_in[layer], preferred_element_type=jnp.float32)
            hidden = (half + half * jnp.tanh(half)).astype(jnp.bfloat16)
            state = state + jnp.dot(
                hidden, mlp_out[layer], preferred_element_type=jnp.float32
            ).reshape(groups, window_len, channels)
        refined = state.reshape(half_rows, channels).astype(jnp.bfloat16)
        term = jnp.dot(matrices[chosen], refined, preferred_element_type=jnp.float32)
        video = term if video is None else video + term
    video = video * scale
    video_out[...] = video.astype(jnp.bfloat16).reshape(slots, tiles * ratio, channels)
    for there in partners:
        send(video_out.at[there], out_ref.at[me], there, video_send, video_recv)
    own = pltpu.make_async_copy(video_out.at[me], out_ref.at[me], own_sem)
    own.start()

    await_bytes(low_out.at[pl.ds(0, slots - 1)], low_send)
    await_bytes(noisy_out.at[pl.ds(0, slots - 1)], noisy_send)
    await_bytes(out_ref.at[pl.ds(0, slots - 1)], video_recv)
    own.wait()
    await_bytes(video_out.at[pl.ds(0, slots - 1)], video_send)


def order_kernel(tiles, video_ref, out_ref, wide, ordered):
    sources, rows, channels = video_ref.shape
    ratio = rows // tiles
    tile_pos = sources * ratio
    wide[...] = video_ref[...].reshape(sources * rows, channels).astype(jnp.float32)
    for t in range(tiles):
        for r in range(ratio):
            ordered[pl.ds(t * tile_pos + r, sources, stride=ratio), :] = wide[
                pl.ds(t * ratio + r, sources, stride=rows), :
            ]
    out_ref[0] = ordered[...].astype(out_ref.dtype)


def split_on_device(*args):
    (lowres, noisy, starts, blend, assign, base_w, cond_w, noise_w, gains, tconv, mlp_in,
     mlp_out) = args
    slots = assign.shape[0]
    tiles = slots // starts.shape[0]
    _, window_len, tile_pos, channels = noisy.shape
    low_pos = lowres.shape[1] // tiles
    ratio = tile_pos // low_pos
    rows = slots * ratio * window_len
    half, full, whole = jnp.bfloat16, jnp.float32, jnp.int32
    dma = pltpu.SemaphoreType.DMA
    video = pl.pallas_call(
        split_kernel,
        out_shape=pltpu.VMEM((slots, tiles * ratio, channels), half),
        in_specs=[pl.BlockSpec(memory_space=pl.ANY)] * len(args),
        out_specs=pl.BlockSpec(memory_space=pltpu.VMEM),
        scratch_shapes=[
            pltpu.VMEM((tiles, low_pos, channels), half),
            pltpu.VMEM(noisy.shape[1:], half),
            pltpu.SMEM(starts.shape, whole),
            pltpu.SMEM(blend.shape, whole),
            pltpu.SMEM(assign.shape, whole),
            pltpu.VMEM(base_w.shape, half),
            pltpu.VMEM(cond_w.shape, half),
            pltpu.VMEM(noise_w.shape, half),
            pltpu.VMEM(gains.shape, full),
            pltpu.VMEM(tconv.shape, full),
            pltpu.VMEM(mlp_in.shape, half),
            pltpu.VMEM(mlp_out.shape, half),
            pltpu.VMEM((slots, tiles, channels), full),
            pltpu.VMEM((slots + 2, tiles, channels), full),
            pltpu.VMEM((window_len * tile_pos, channels), full),
            pltpu.VMEM((slots, ratio * window_len, channels), half),
            pltpu.VMEM((2, slots // 2, ratio * window_len, channels), half),
            pltpu.VMEM((tiles * slots, channels), full),
            pltpu.VMEM((tiles, slots - window_len + 1, window_len, channels), full),
            pltpu.VMEM((2, slots // 2, 1, window_len, channels), full),
            pltpu.VMEM((slots, tiles * ratio, channels), half),
            pltpu.VMEM((2, slots * tiles * ratio, rows // 2), half),
            dma((len(args),)), dma, dma, dma, dma((2,)), dma, dma, dma,
        ],
        compiler_params=pltpu.CompilerParams(
            collective_id=0, has_side_effects=True, vmem_limit_bytes=60 * 1024 * 1024
        ),
    )(lowres.reshape(tiles, low_pos, channels), *args[1:])
    return pl.pallas_call(
        functools.partial(order_kernel, tiles),
        out_shape=jax.ShapeDtypeStruct((1, tiles * tile_pos, channels), half),
        in_specs=[pl.BlockSpec(memory_space=pltpu.VMEM)],
        out_specs=pl.BlockSpec(memory_space=pltpu.VMEM),
        scratch_shapes=[
            pltpu.VMEM((tiles * tile_pos, channels), full),
            pltpu.VMEM((tiles * tile_pos, channels), full),
        ],
        compiler_params=pltpu.CompilerParams(vmem_limit_bytes=16 * 1024 * 1024),
    )(video)


def on_device(*args):
    lowres, noisy, starts, _, assign = args[:5]
    slots = assign.shape[0]
    tiles = slots // starts.shape[0]
    low_pos = lowres.shape[1] // tiles
    ratio = noisy.shape[2] // low_pos
    if (
        low_pos == slots and slots % 2 == 0 and tiles <= SUBLANES and noisy.shape[1] == SUBLANES
        and (tiles * ratio) % 16 == 0
    ):
        return split_on_device(*args)
    return slot_on_device(2, *args)


def solution(mesh):
    in_specs = (
        P(("groups", AXIS), None, None),
        P(("groups", AXIS), None, None, None),
        P("groups"),
        P("groups", None),
        P("groups"),
        P(),
        P(),
        P(),
        P(),
        P(),
        P(),
        P(),
    )
    out_specs = P(("groups", AXIS), None, None)
    return jax.shard_map(
        on_device,
        mesh=mesh, in_specs=in_specs, out_specs=out_specs, check_vma=False
    )
```
